32 devices in a mesh: own: 2 (over x), dom: 16 (over z, y, core).
Axes of the slice: x: 2, y: 2, z: 4, core: 2. Of those that a mesh axis runs over, the one named last changes fastest.
Arguments:
- background: bfloat16 [64, 6, 4096], P(('own', 'dom')), may hold values from -6 to 6
- storm_track: float32 [2, 5], replicated, may hold values from 0.02 to 1638.4, as said below
- need_tiles: int32 [32, 8], P(('own', 'dom')), may hold values from 0 to 63, as said below
- node_cells: int32 [256, 1024], P(('own', 'dom')), may hold values from 0 to 4030, as said below
- node_fracs: float32 [2, 256, 1024], P(None, ('own', 'dom')), may hold values from 0 to 1
- slot_count: int32 [256], P(('own', 'dom')), may hold values from 256 to 1024
- elevation: float32 [2, 131072], P('own', 'dom'), may hold values from 0 to 2
- bed_level: float32 [2, 131072], P('own', 'dom'), may hold values from -1 to 1.5
Outputs:
- forcing: bfloat16 [256, 6, 1024], P(('own', 'dom'))
- surge_level: float32 [2, 131072], P('own', 'dom')
The draws below stay inside these ranges and needn't reach their ends.
Inputs may be any that keep to these rules, and one draw needn't show every extreme that they name: `need_tiles`: entries k * 4 to (k + 1) * 4 - 1 of a row name tiles of band k (tiles k * 32 to (k + 1) * 32 - 1); within a row the numbers (tile % 32) // 2 are all different. `node_cells`: value // 64 and value % 64 are both at most 62. `storm_track`: row k: centre column and row in cells, pressure deficit, radius of maximum wind in cells, shape exponent; all positive.
All inputs are finite; a program needn't handle non-finite values.
Results may differ from the reference program's by a relative error of at most 0.0023.
The reference program's roundings to bfloat16 on the way count: a program that leaves them out, or rounds other values in their place, can miss the bound.
Values may be sent and summed in bfloat16 or wider, within the bound.
A program may use at most 64 MiB of HBM per device.

```python
import jax
import jax.numpy as jnp
from jax import lax

TILE = 64
TCOLS = 32
TILES_DEV = 2
FIELDS = 6
K_B = 4
NPS = 1024
SWEEPS = 4
NEED = 8
BAND = 32
TILES = 64
GRID_ROWS = 128
GRID_COLS = 2048
SLOTS = 256
CHAIN = 131072
N_OWN = 2
N_DOM = 16
DEVICES = 32


def draw_storm_track(key, part):
    streams = jax.random.split(key, 5)
    centre_col = jax.random.uniform(streams[0], (2,), jnp.float32, 0.2, 0.8) * GRID_COLS
    centre_row = jax.random.uniform(streams[1], (2,), jnp.float32, 0.2, 0.8) * GRID_ROWS
    deficit = jax.random.uniform(streams[2], (2,), jnp.float32, 0.5, 1.5)
    max_radius = jax.random.uniform(streams[3], (2,), jnp.float32, 0.02, 0.06) * GRID_COLS
    exponent = jax.random.uniform(streams[4], (2,), jnp.float32, 1.0, 2.0)
    return jnp.stack([centre_col, centre_row, deficit, max_radius, exponent], axis=1)


def draw_need_tiles(key, part):
    streams = jax.random.split(key, DEVICES)

    def one_row(stream):
        first, second = jax.random.split(stream)
        holder_slots = jax.random.permutation(first, N_DOM)[:NEED].astype(jnp.int32)
        band_index = jnp.arange(NEED, dtype=jnp.int32) // K_B
        within_holder = jax.random.randint(second, (NEED,), 0, TILES_DEV, dtype=jnp.int32)
        return band_index * BAND + holder_slots * TILES_DEV + within_holder
    return jax.vmap(one_row)(streams).astype(jnp.int32)


def draw_node_cells(key, part):
    first, second = jax.random.split(key)
    row_first = jax.random.randint(first, (SLOTS, NPS), 0, TILE - 1, dtype=jnp.int32)
    col_first = jax.random.randint(second, (SLOTS, NPS), 0, TILE - 1, dtype=jnp.int32)
    return (row_first * TILE + col_first).astype(jnp.int32)


def plant(drawn, stream_key, least, top_value):
    dims = drawn.shape
    place = [jax.random.randint(jax.random.fold_in(stream_key, axis), (), 0, dims[axis]) for axis in range(len(dims))]
    drawn = drawn.at[tuple(place)].set(least)
    longest = dims.index(max(dims))
    place[longest] = (place[longest] + 1) % dims[longest]
    return drawn.at[tuple(place)].set(top_value)


def block_scale(rng, shape, shards, smallest, top_value):
    def one(dim, blocks):
        draws = jax.random.uniform(jax.random.fold_in(jax.random.fold_in(rng, 6), dim), (blocks,), jnp.float32, smallest / len(shards), top_value / len(shards))
        return jnp.repeat(jnp.exp(draws), shape[dim] // blocks).reshape((-1,) + (1,) * (len(shape) - dim - 1))

    loudness = one(*shards[0])
    for cut in shards[1:]:
        loudness = loudness * one(*cut)
    return loudness


def noise(key, shape, scale, reach, pieces=(), held_as=jnp.bfloat16):
    values = jax.random.normal(key, shape, jnp.float32) * scale
    if len(pieces) > 0:
        values = block_scale(key, shape, pieces, -0.22, 0.18) * values
    return jnp.clip(values, min=-reach, max=reach).astype(held_as)


def setup_inputs(seed: int = 0) -> dict:
    arg_keys = jax.random.split(jax.random.key(seed), 9)
    background = noise(arg_keys[0], (TILES, FIELDS, TILE * TILE), 1.0, 6.0, ((0, 32),))
    storm_track = draw_storm_track(jax.random.fold_in(arg_keys[8], 71), 0)
    need_tiles = draw_need_tiles(jax.random.fold_in(arg_keys[8], 71), 0)
    node_cells = draw_node_cells(jax.random.fold_in(arg_keys[8], 71), 0)
    node_fracs = jnp.clip(1.0 * jax.random.uniform(arg_keys[4], (2, SLOTS, NPS), jnp.float32) ** block_scale(arg_keys[4], (2, SLOTS, NPS), ((1, 32),), -0.2, 0.2), 0.0, 1.0)
    slot_count = plant(jax.random.randint(arg_keys[5], (SLOTS,), NPS // 4, NPS + 1), jax.random.fold_in(arg_keys[5], 1), NPS // 4, NPS).astype(jnp.int32)
    elevation = jnp.clip(2.0 * jax.random.uniform(arg_keys[6], (N_OWN, CHAIN), jnp.float32) ** block_scale(arg_keys[6], (N_OWN, CHAIN), ((0, 2), (1, 16)), -0.2, 0.2), 0.0, 2.0)
    bed_level = jnp.clip(-1.0 + 2.5 * jax.random.uniform(arg_keys[7], (N_OWN, CHAIN), jnp.float32) ** block_scale(arg_keys[7], (N_OWN, CHAIN), ((0, 2), (1, 16)), -0.2, 0.2), -1.0, 1.5)
    return dict(background=background, storm_track=storm_track, need_tiles=need_tiles, node_cells=node_cells, node_fracs=node_fracs, slot_count=slot_count, elevation=elevation, bed_level=bed_level)


KAPPA = 0.08

def holland(tile_index, background, storm_track):
    cell_index = jnp.arange(TILE * TILE, dtype=jnp.int32)
    cell_row = (cell_index // TILE).astype(jnp.float32)
    cell_col = (cell_index % TILE).astype(jnp.float32)
    tile_row = (tile_index // TCOLS).astype(jnp.float32)
    tile_col = (tile_index % TCOLS).astype(jnp.float32)
    north_cell = tile_row[:, None] * TILE + cell_row[None, :]
    east_cell = tile_col[:, None] * TILE + cell_col[None, :]
    fields = []
    for time_level in range(2):
        offset_x = east_cell - storm_track[time_level, 0]
        offset_y = north_cell - storm_track[time_level, 1]
        radius = jnp.sqrt(offset_x * offset_x + offset_y * offset_y + 1.0)
        radial_ratio = jnp.exp(storm_track[time_level, 4] * jnp.log(storm_track[time_level, 3] / radius))
        pressure_decay = jnp.exp(-radial_ratio)
        wind_speed = jnp.sqrt(storm_track[time_level, 4] * storm_track[time_level, 2] * radial_ratio * pressure_decay)
        fields.append(-wind_speed * offset_y / radius)
        fields.append(wind_speed * offset_x / radius)
        fields.append(-storm_track[time_level, 2] * (1.0 - pressure_decay))
    return (background.astype(jnp.float32) + jnp.stack(fields, axis=1)).astype(jnp.bfloat16)

def interpolate(tile_data, cell_index, fractions, counts):
    flat = tile_data.astype(jnp.float32)

    def corner(offset):
        index = (cell_index + offset).astype(jnp.int32)
        return jnp.take_along_axis(flat, index[:, None, :], axis=2)
    near_weight = lax.optimization_barrier((1.0 - fractions[0]).astype(jnp.bfloat16)).astype(jnp.float32)
    far_weight = lax.optimization_barrier(fractions[0].astype(jnp.bfloat16)).astype(jnp.float32)
    upper_row = corner(0) * near_weight[:, None, :] + corner(1) * far_weight[:, None, :]
    bottom = corner(TILE) * near_weight[:, None, :] + corner(TILE + 1) * far_weight[:, None, :]
    north_frac = fractions[1][:, None, :]
    node_value = (1.0 - north_frac) * upper_row + north_frac * bottom
    live = jnp.arange(NPS, dtype=jnp.int32)[None, :] < counts[:, None]
    return jnp.where(live[:, None, :], node_value, jnp.float32(0.0))

def flux_sweep(elevation, bed_level):
    surface = elevation
    for sweep_step in range(SWEEPS):
        wet_depth = jnp.maximum(surface - bed_level, 0.0)
        slope_drop = surface[:, :-1] - surface[:, 1:]
        upwind = jnp.where(slope_drop >= 0.0, wet_depth[:, :-1], wet_depth[:, 1:])
        face_flux = KAPPA * upwind * slope_drop
        wall_zero = jnp.zeros((surface.shape[0], 1), jnp.float32)
        faces = jnp.concatenate([wall_zero, face_flux, wall_zero], axis=1)
        surface = surface - (faces[:, 1:] - faces[:, :-1])
    return surface

def reference(background, storm_track, need_tiles, node_cells, node_fracs, slot_count, elevation, bed_level):
    forcing_grid = holland(jnp.arange(TILES, dtype=jnp.int32), background, storm_track)
    cell_parts = node_cells.reshape(DEVICES, NEED, NPS)
    frac_parts = jnp.moveaxis(node_fracs.reshape(2, DEVICES, NEED, NPS), 1, 0)
    count_parts = slot_count.reshape(DEVICES, NEED)

    def device_part(packed):
        wanted, cell_part, frac_part, count_part = packed
        return interpolate(jnp.take(forcing_grid, wanted.astype(jnp.int32), axis=0), cell_part, frac_part, count_part)
    values = lax.map(device_part, (need_tiles, cell_parts, frac_parts, count_parts))
    forcing = values.reshape(SLOTS, FIELDS, NPS).astype(jnp.bfloat16)
    pressure = values[:, :, 5, :].reshape(N_OWN, CHAIN)
    surface = flux_sweep(elevation, bed_level)
    surge_level = surface - 0.5 * pressure * jnp.clip(surface - bed_level, 0.0, 1.0)
    return (forcing, surge_level)
```

```python
import functools

import jax
import jax.numpy as jnp
from jax import lax
from jax.experimental import pallas as pl
from jax.experimental.pallas import tpu as pltpu
from jax.sharding import PartitionSpec as P

TILE = 64
TCOLS = 32
SWEEPS = 4
KAPPA = 0.08
LANES = 128
HALO = 8


def kernel(
    groups, holders,
    storm_ref, need_ref, count_ref, back_ref, cells_ref, fracs_ref, elev_ref, bed_ref,
    forcing_ref, surge_ref,
    grid_ref, field_ref, data_ref, node_out_ref, need_out_ref, need_in_ref, need_smem,
    colw_ref, roww_ref, surf_ref, ground_ref, press_ref, res_out_ref, res_in_ref,
    ring_send, ring_recv, sib_send, sib_recv, halo_send, halo_recv,
    node_send, node_recv, need_send, need_recv, need_local, res_send, res_recv,
):
    own = lax.axis_index("own")
    dom = lax.axis_index("dom")
    tiles_dev, fields, cell_count = back_ref.shape
    slots, positions = cells_ref.shape
    per_band = slots // groups
    pairs = cell_count // LANES
    chips = holders // 2
    half = chips // 2
    band = tiles_dev * holders

    core = dom % 2
    chip = dom // 2
    odd = chip % 2
    place = (chip // 2) * (1 - odd) + (chips - 1 - chip // 2) * odd

    def device_at(where, which_core):
        where = (where + chips) % chips
        back = where // half
        at_chip = (2 * where) * (1 - back) + (2 * (chips - 1 - where) + 1) * back
        return at_chip * 2 + which_core

    right = device_at(place + 1, core)
    left = device_at(place - 1, core)
    sibling = chip * 2 + 1 - core
    after = (dom + 1) % holders
    before = (dom + holders - 1) % holders

    barrier = pltpu.get_barrier_semaphore()
    for neighbour in (right, left, sibling, after, before):
        pl.semaphore_signal(barrier, inc=1, device_id={"dom": neighbour})
    for j in range(1, groups):
        pl.semaphore_signal(barrier, inc=1, device_id={"own": (own + j) % groups})

    pair_index = lax.broadcasted_iota(jnp.int32, (pairs, LANES), 0)
    lane_index = lax.broadcasted_iota(jnp.int32, (pairs, LANES), 1)
    cell_row = (pair_index * (LANES // TILE) + lane_index // TILE).astype(jnp.float32)
    cell_col = (lane_index % TILE).astype(jnp.float32)
    for t in range(tiles_dev):
        for p in range(pairs):
            field_ref[pl.ds(p, fields, stride=pairs), :] = back_ref[
                t, :, p * LANES : (p + 1) * LANES
            ].astype(jnp.float32)
        tile = own * band + dom * tiles_dev + t
        north = (tile // TCOLS * TILE).astype(jnp.float32) + cell_row
        east = (tile % TCOLS * TILE).astype(jnp.float32) + cell_col
        mine = grid_ref.at[dom * tiles_dev + t]
        for k in range(2):
            offset_x = east - storm_ref[k, 0]
            offset_y = north - storm_ref[k, 1]
            deficit = storm_ref[k, 2]
            shape = storm_ref[k, 4]
            radius = jnp.sqrt(offset_x * offset_x + offset_y * offset_y + 1.0)
            ratio = jnp.exp(shape * jnp.log(storm_ref[k, 3] / radius))
            decay = jnp.exp(-ratio)
            speed = jnp.sqrt(shape * deficit * ratio * decay)
            added = (
                -speed * offset_y / radius,
                speed * offset_x / radius,
                -deficit * (1.0 - decay),
            )
            for m, term in enumerate(added):
                rows = pl.ds((3 * k + m) * pairs, pairs)
                mine[rows, :] = (field_ref[rows, :] + term).astype(jnp.bfloat16)

    pl.semaphore_wait(barrier, 5 + groups - 1)

    def tile_of(where, which_core, t):
        return grid_ref.at[device_at(where, which_core) * tiles_dev + t]

    def ring_copy(way, far, t):
        where = place - far + 1 if way == 0 else place + far - 1
        ref = tile_of(where, core, t)
        return pltpu.make_async_remote_copy(
            src_ref=ref, dst_ref=ref,
            send_sem=ring_send.at[way, far - 1, t], recv_sem=ring_recv.at[way, far - 1, t],
            device_id={"dom": right if way == 0 else left},
        )

    def ring_arrival(way, far, t):
        where = place - far if way == 0 else place + far
        ref = tile_of(where, core, t)
        return pltpu.make_async_remote_copy(
            src_ref=ref, dst_ref=ref,
            send_sem=ring_send.at[way, far - 1, t], recv_sem=ring_recv.at[way, far - 1, t],
            device_id={"dom": right if way == 0 else left},
        )

    def sibling_copy(way, far, t, which_core):
        where = place - far if way == 0 else place + far
        ref = tile_of(where, which_core, t)
        return pltpu.make_async_remote_copy(
            src_ref=ref, dst_ref=ref,
            send_sem=sib_send.at[way, far, t], recv_sem=sib_recv.at[way, far, t],
            device_id={"dom": sibling},
        )

    def reach(way, t):
        return half if t % 2 == way else half - 1

    sent = []

    def start(copy):
        copy.start()
        sent.append(copy)

    first = [(way, (way + s) % tiles_dev) for s in range(tiles_dev) for way in range(2)]
    for way, t in first:
        if reach(way, t) >= 1:
            start(ring_copy(way, 1, t))
    for t in range(tiles_dev):
        start(sibling_copy(0, 0, t, core))

    length = elev_ref.shape[0]
    ends = ((after, length - HALO, 0, 0), (before, 0, HALO + length, 1))
    halo = []
    for target, source_row, target_row, side in ends:
        for m, (source, target_ref) in enumerate(((elev_ref, surf_ref), (bed_ref, ground_ref))):
            copy = pltpu.make_async_remote_copy(
                src_ref=source.at[pl.ds(source_row, HALO)],
                dst_ref=target_ref.at[pl.ds(target_row, HALO)],
                send_sem=halo_send.at[side, m], recv_sem=halo_recv.at[side, m],
                device_id={"dom": target},
            )
            start(copy)
            halo.append(copy)

    live_index = lax.broadcasted_iota(jnp.int32, (1, positions), 1)
    row_index = lax.broadcasted_iota(jnp.int32, (8, LANES), 0)

    def node_rows(j, target):
        group = (own + j) % groups
        for i in range(per_band):
            slot = group * per_band + i
            live = live_index < count_ref[slot]
            north_frac = fracs_ref[1, pl.ds(slot, 1), :]
            target[pl.ds(i, 1), :] = cells_ref[pl.ds(slot, 1), :].astype(jnp.float32)
            target[pl.ds(per_band + i, 1), :] = fracs_ref[0, pl.ds(slot, 1), :]
            target[pl.ds(2 * per_band + i, 1), :] = jnp.where(live, 1.0 - north_frac, 0.0)
            target[pl.ds(3 * per_band + i, 1), :] = jnp.where(live, north_frac, 0.0)

    asked = []
    for j in range(1, groups):
        group = (own + j) % groups
        node_rows(j, node_out_ref.at[j - 1])
        wanted = jnp.zeros((8, LANES), jnp.int32)
        for i in range(per_band):
            wanted = jnp.where(row_index == i, need_ref[0, group * per_band + i], wanted)
        need_out_ref[j - 1] = wanted
        node = pltpu.make_async_remote_copy(
            src_ref=node_out_ref.at[j - 1], dst_ref=data_ref.at[j],
            send_sem=node_send.at[j], recv_sem=node_recv.at[j],
            device_id={"own": group},
        )
        start(node)
        need = pltpu.make_async_remote_copy(
            src_ref=need_out_ref.at[j - 1], dst_ref=need_in_ref.at[j - 1],
            send_sem=need_send.at[j], recv_sem=need_recv.at[j],
            device_id={"own": group},
        )
        start(need)
        asked.append((node, need))
    node_rows(0, data_ref.at[0])

    col_index = lax.broadcasted_iota(jnp.int32, (TILE, positions), 0)
    even_index = lax.broadcasted_iota(jnp.int32, (pairs, positions), 0) * 2

    def weights(j, i):
        cells = data_ref[j, pl.ds(i, 1), :].astype(jnp.int32)
        east_frac = data_ref[j, pl.ds(per_band + i, 1), :]
        upper = data_ref[j, pl.ds(2 * per_band + i, 1), :]
        lower = data_ref[j, pl.ds(3 * per_band + i, 1), :]
        col_first = cells % TILE
        row_first = cells // TILE
        colw_ref[j * per_band + i] = jnp.where(
            col_index == col_first, 1.0 - east_frac,
            jnp.where(col_index == col_first + 1, east_frac, 0.0),
        ).astype(jnp.bfloat16)
        for h in range(2):
            row = even_index + h
            roww_ref[j * per_band + i, h] = jnp.where(
                row == row_first, upper, jnp.where(row == row_first + 1, lower, 0.0)
            )

    def await_asked(j):
        node, need = asked[j - 1]
        need.wait_recv()
        local = pltpu.make_async_copy(
            need_in_ref.at[j - 1], need_smem.at[j - 1], need_local.at[j]
        )
        local.start()
        node.wait_recv()
        local.wait()

    def sweep():
        surf_ref[pl.ds(HALO, length), :] = elev_ref[...]
        ground_ref[pl.ds(HALO, length), :] = bed_ref[...]
        for copy in halo:
            copy.wait_recv()
        surface = surf_ref[...]
        ground = ground_ref[...]
        rows = length + 2 * HALO
        row = lax.broadcasted_iota(jnp.int32, (rows, LANES), 0)
        lane = lax.broadcasted_iota(jnp.int32, (rows, LANES), 1)
        wall = ((row == HALO - 1) & (lane == LANES - 1) & (dom == 0)) | (
            (row == HALO + length - 1) & (lane == LANES - 1) & (dom == holders - 1)
        )

        def shifted(values, by):
            turned = pltpu.roll(values, by % LANES, 1)
            other = pltpu.roll(turned, by % rows, 0)
            edge = lane == (0 if by == 1 else LANES - 1)
            return jnp.where(edge, other, turned)

        for _ in range(SWEEPS):
            wet = jnp.maximum(surface - ground, 0.0)
            drop = surface - shifted(surface, -1)
            upwind = jnp.where(drop >= 0.0, wet, shifted(wet, -1))
            flux = jnp.where(wall, 0.0, KAPPA * upwind * drop)
            surface = surface - (flux - shifted(flux, 1))
        surf_ref[...] = surface

    work = [functools.partial(weights, 0, i) for i in range(per_band)]
    for j in range(1, groups):
        work.append(functools.partial(await_asked, j))
        work += [functools.partial(weights, j, i) for i in range(per_band)]
    work.append(sweep)

    events = [
        (way, far, t)
        for far in range(1, half + 1)
        for way, t in first
        if far <= reach(way, t)
    ]
    done = 0
    for n, (way, far, t) in enumerate(events):
        until = (n + 1) * len(work) // len(events)
        for item in work[done:until]:
            item()
        done = until
        ring_arrival(way, far, t).wait_recv()
        if far < reach(way, t):
            start(ring_copy(way, far + 1, t))
        start(sibling_copy(way, far, t, core))
    for t in range(tiles_dev):
        sibling_copy(0, 0, t, 1 - core).wait_recv()
    for way, far, t in events:
        sibling_copy(way, far, t, 1 - core).wait_recv()

    chunk = 256

    def node_values(j, i, tile):
        cells = grid_ref[lax.rem(tile, band)]
        slot = j * per_band + i
        parts = []
        for n in range(positions // chunk):
            cut = pl.ds(n * chunk, chunk)
            total = None
            for h in range(2):
                spread = jnp.dot(
                    cells[:, h * TILE : (h + 1) * TILE], colw_ref[slot, :, cut],
                    preferred_element_type=jnp.float32,
                )
                part = spread.reshape(fields, pairs, chunk) * roww_ref[slot, h, :, cut][None]
                total = part if total is None else total + part
            parts.append(jnp.sum(total, axis=1))
        return jnp.concatenate(parts, axis=1)

    def keep_pressure(slot, pressure):
        for m in range(positions // LANES):
            press_ref[pl.ds(slot * (positions // LANES) + m, 1), :] = pressure[
                :, m * LANES : (m + 1) * LANES
            ]

    answers = []
    for j in range(1, groups):
        for m in range(per_band // 2):
            rows = []
            for i in (2 * m, 2 * m + 1):
                value = node_values(j, i, need_smem[j - 1, i, 0])
                pressure = value[fields - 1 : fields]
                rest = pressure - pressure.astype(jnp.bfloat16).astype(jnp.float32)
                rows += [value, rest, jnp.zeros((8 - fields - 1, positions), jnp.float32)]
            res_out_ref[j - 1, m] = jnp.concatenate(rows, axis=0).astype(jnp.bfloat16)
            copy = pltpu.make_async_remote_copy(
                src_ref=res_out_ref.at[j - 1, m], dst_ref=res_in_ref.at[j - 1, m],
                send_sem=res_send.at[j - 1, m], recv_sem=res_recv.at[j - 1, m],
                device_id={"own": (own + groups - j) % groups},
            )
            start(copy)
            answers.append((j, m, copy))
    for i in range(per_band):
        slot = own * per_band + i
        value = node_values(0, i, need_ref[0, slot])
        forcing_ref[slot] = value.astype(jnp.bfloat16)
        keep_pressure(slot, value[fields - 1 : fields])
    for j, m, copy in answers:
        copy.wait_recv()
        got = res_in_ref[j - 1, m].astype(jnp.float32)
        for i in range(2):
            slot = (own + j) % groups * per_band + 2 * m + i
            value = got[8 * i : 8 * i + fields]
            forcing_ref[slot] = value.astype(jnp.bfloat16)
            keep_pressure(
                slot, got[8 * i + fields - 1 : 8 * i + fields] + got[8 * i + fields : 8 * i + fields + 1]
            )
    surface = surf_ref[pl.ds(HALO, length), :]
    surge_ref[...] = surface - 0.5 * press_ref[...] * jnp.clip(surface - bed_ref[...], 0.0, 1.0)
    for copy in sent:
        copy.wait_send()


def shards(
    background, storm_track, need_tiles, node_cells, node_fracs, slot_count, elevation, bed_level
):
    groups = lax.axis_size("own")
    holders = lax.axis_size("dom")
    tiles_dev, fields, cell_count = background.shape
    slots, positions = node_cells.shape
    per_band = slots // groups
    chips = holders // 2
    half = chips // 2
    pairs = cell_count // LANES
    length = elevation.shape[1] // LANES
    others = max(groups - 1, 1)
    vmem = pl.BlockSpec(memory_space=pltpu.VMEM)
    smem = pl.BlockSpec(memory_space=pltpu.SMEM)
    dma = pltpu.SemaphoreType.DMA
    forcing, surge = pl.pallas_call(
        functools.partial(kernel, groups, holders),
        out_shape=(
            jax.ShapeDtypeStruct((slots, fields, positions), jnp.bfloat16),
            jax.ShapeDtypeStruct((length, LANES), jnp.float32),
        ),
        in_specs=[smem] * 3 + [vmem] * 5,
        out_specs=(vmem, vmem),
        scratch_shapes=[
            pltpu.VMEM((tiles_dev * holders, fields * pairs, LANES), jnp.bfloat16),
            pltpu.VMEM((fields * pairs, LANES), jnp.float32),
            pltpu.VMEM((groups, 4 * per_band, positions), jnp.float32),
            pltpu.VMEM((others, 4 * per_band, positions), jnp.float32),
            pltpu.VMEM((others, 8, LANES), jnp.int32),
            pltpu.VMEM((others, 8, LANES), jnp.int32),
            pltpu.SMEM((others, 8, LANES), jnp.int32),
            pltpu.VMEM((slots, TILE, positions), jnp.bfloat16),
            pltpu.VMEM((slots, 2, pairs, positions), jnp.float32),
            pltpu.VMEM((length + 2 * HALO, LANES), jnp.float32),
            pltpu.VMEM((length + 2 * HALO, LANES), jnp.float32),
            pltpu.VMEM((length, LANES), jnp.float32),
            pltpu.VMEM((others, per_band // 2, 16, positions), jnp.bfloat16),
            pltpu.VMEM((others, per_band // 2, 16, positions), jnp.bfloat16),
            dma((2, half, tiles_dev)), dma((2, half, tiles_dev)),
            dma((2, half + 1, tiles_dev)), dma((2, half + 1, tiles_dev)),
            dma((2, 2)), dma((2, 2)),
            dma((groups,)), dma((groups,)),
            dma((groups,)), dma((groups,)), dma((groups,)),
            dma((others, per_band // 2)), dma((others, per_band // 2)),
        ],
        compiler_params=pltpu.CompilerParams(
            collective_id=0, has_side_effects=True, vmem_limit_bytes=48 * 1024 * 1024
        ),
    )(
        storm_track, need_tiles, slot_count, background, node_cells, node_fracs,
        elevation.reshape(length, LANES), bed_level.reshape(length, LANES),
    )
    return forcing, surge.reshape(1, -1)


def solution(mesh):
    placed = (
        P(("own", "dom"), None, None),
        P(),
        P(("own", "dom"), None),
        P(("own", "dom"), None),
        P(None, ("own", "dom"), None),
        P(("own", "dom")),
        P("own", "dom"),
        P("own", "dom"),
    )
    return jax.shard_map(
        shards,
        mesh=mesh,
        in_specs=placed,
        out_specs=(P(("own", "dom"), None, None), P("own", "dom")),
        check_vma=False,
    )
```

```python
import functools

import jax
import jax.numpy as jnp
from jax import lax
from jax.experimental import pallas as pl
from jax.experimental.pallas import tpu as pltpu
from jax.sharding import PartitionSpec as P

TILE = 64
TCOLS = 32
SWEEPS = 4
KAPPA = 0.08
LANES = 128
HALO = 8


def kernel(
    groups, holders,
    storm_ref, need_ref, count_ref, back_ref, cells_ref, fracs_ref, elev_ref, bed_ref,
    forcing_ref, surge_ref,
    grid_ref, field_ref, data_ref, node_out_ref, need_out_ref, need_in_ref, need_smem,
    colw_ref, roww_ref, surf_ref, ground_ref, press_ref, value_ref, res_out_ref, res_in_ref,
    ring_send, ring_recv, sib_send, sib_recv, halo_send, halo_recv,
    node_send, node_recv, need_send, need_recv, need_local, res_send, res_recv,
):
    own = lax.axis_index("own")
    dom = lax.axis_index("dom")
    tiles_dev = grid_ref.shape[0] // holders
    fields, slots, positions = forcing_ref.shape
    pairs = grid_ref.shape[1] // fields
    per_band = slots // groups
    chips = holders // 2
    half = chips // 2
    band = tiles_dev * holders

    core = dom % 2
    chip = dom // 2
    odd = chip % 2
    place = (chip // 2) * (1 - odd) + (chips - 1 - chip // 2) * odd

    def device_at(where, which_core):
        where = (where + chips) % chips
        back = where // half
        at_chip = (2 * where) * (1 - back) + (2 * (chips - 1 - where) + 1) * back
        return at_chip * 2 + which_core

    right = device_at(place + 1, core)
    left = device_at(place - 1, core)
    sibling = chip * 2 + 1 - core
    after = (dom + 1) % holders
    before = (dom + holders - 1) % holders

    barrier = pltpu.get_barrier_semaphore()
    for neighbour in (right, left, sibling, after, before):
        pl.semaphore_signal(barrier, inc=1, device_id={"dom": neighbour})
    for j in range(1, groups):
        pl.semaphore_signal(barrier, inc=1, device_id={"own": (own + j) % groups})

    deep = pairs * tiles_dev
    deep_index = lax.broadcasted_iota(jnp.int32, (deep, LANES), 0)
    lane_index = lax.broadcasted_iota(jnp.int32, (deep, LANES), 1)
    tile = own * band + dom * tiles_dev + deep_index % tiles_dev
    cell_row = deep_index // tiles_dev * (LANES // TILE) + lane_index // TILE
    north = (tile // TCOLS * TILE + cell_row).astype(jnp.float32)
    east = (tile % TCOLS * TILE + lane_index % TILE).astype(jnp.float32)
    for k in range(2):
        offset_x = east - storm_ref[k, 0]
        offset_y = north - storm_ref[k, 1]
        deficit = storm_ref[k, 2]
        shape = storm_ref[k, 4]
        radius = jnp.sqrt(offset_x * offset_x + offset_y * offset_y + 1.0)
        ratio = jnp.exp(shape * jnp.log(storm_ref[k, 3] / radius))
        decay = jnp.exp(-ratio)
        speed = jnp.sqrt(shape * deficit * ratio * decay) / radius
        added = (-speed * offset_y, speed * offset_x, -deficit * (1.0 - decay))
        for m, term in enumerate(added):
            rows = pl.ds((3 * k + m) * deep, deep)
            field_ref[rows, :] = back_ref[rows, :].astype(jnp.float32) + term
    for t in range(tiles_dev):
        grid_ref[dom * tiles_dev + t] = field_ref[
            pl.ds(t, fields * pairs, stride=tiles_dev), :
        ].astype(jnp.bfloat16)

    pl.semaphore_wait(barrier, 5 + groups - 1)

    def tile_of(where, which_core, t):
        return grid_ref.at[device_at(where, which_core) * tiles_dev + t]

    def ring_copy(way, far, t):
        where = place - far + 1 if way == 0 else place + far - 1
        ref = tile_of(where, core, t)
        return pltpu.make_async_remote_copy(
            src_ref=ref, dst_ref=ref,
            send_sem=ring_send.at[way, far - 1, t], recv_sem=ring_recv.at[way, far - 1, t],
            device_id={"dom": right if way == 0 else left},
        )

    def ring_arrival(way, far, t):
        where = place - far if way == 0 else place + far
        ref = tile_of(where, core, t)
        return pltpu.make_async_remote_copy(
            src_ref=ref, dst_ref=ref,
            send_sem=ring_send.at[way, far - 1, t], recv_sem=ring_recv.at[way, far - 1, t],
            device_id={"dom": right if way == 0 else left},
        )

    def sibling_copy(way, far, t, which_core):
        where = place - far if way == 0 else place + far
        ref = tile_of(where, which_core, t)
        return pltpu.make_async_remote_copy(
            src_ref=ref, dst_ref=ref,
            send_sem=sib_send.at[way, far, t], recv_sem=sib_recv.at[way, far, t],
            device_id={"dom": sibling},
        )

    def reach(way, t):
        return half if t % 2 == way else half - 1

    sent = []

    def start(copy):
        copy.start()
        sent.append(copy)

    first = [(way, (way + s) % tiles_dev) for s in range(tiles_dev) for way in range(2)]
    for way, t in first:
        if reach(way, t) >= 1:
            start(ring_copy(way, 1, t))
    for t in range(tiles_dev):
        start(sibling_copy(0, 0, t, core))

    length = elev_ref.shape[0]
    ends = ((after, length - HALO, 0, 0), (before, 0, HALO + length, 1))
    halo = []
    for target, source_row, target_row, side in ends:
        for m, (source, target_ref) in enumerate(((elev_ref, surf_ref), (bed_ref, ground_ref))):
            copy = pltpu.make_async_remote_copy(
                src_ref=source.at[pl.ds(source_row, HALO)],
                dst_ref=target_ref.at[pl.ds(target_row, HALO)],
                send_sem=halo_send.at[side, m], recv_sem=halo_recv.at[side, m],
                device_id={"dom": target},
            )
            start(copy)
            halo.append(copy)

    live_index = lax.broadcasted_iota(jnp.int32, (1, positions), 1)
    row_index = lax.broadcasted_iota(jnp.int32, (8, LANES), 0)

    def node_rows(j, target):
        group = (own + j) % groups
        for i in range(per_band):
            slot = group * per_band + i
            live = live_index < count_ref[slot]
            north_frac = fracs_ref[1, pl.ds(slot, 1), :]
            target[pl.ds(i, 1), :] = cells_ref[pl.ds(slot, 1), :].astype(jnp.float32)
            target[pl.ds(per_band + i, 1), :] = fracs_ref[0, pl.ds(slot, 1), :]
            target[pl.ds(2 * per_band + i, 1), :] = jnp.where(live, 1.0 - north_frac, 0.0)
            target[pl.ds(3 * per_band + i, 1), :] = jnp.where(live, north_frac, 0.0)

    asked = []
    for j in range(1, groups):
        group = (own + j) % groups
        node_rows(j, node_out_ref.at[j - 1])
        wanted = jnp.zeros((8, LANES), jnp.int32)
        for i in range(per_band):
            wanted = jnp.where(row_index == i, need_ref[0, group * per_band + i], wanted)
        need_out_ref[j - 1] = wanted
        node = pltpu.make_async_remote_copy(
            src_ref=node_out_ref.at[j - 1], dst_ref=data_ref.at[j],
            send_sem=node_send.at[j], recv_sem=node_recv.at[j],
            device_id={"own": group},
        )
        start(node)
        need = pltpu.make_async_remote_copy(
            src_ref=need_out_ref.at[j - 1], dst_ref=need_in_ref.at[j - 1],
            send_sem=need_send.at[j], recv_sem=need_recv.at[j],
            device_id={"own": group},
        )
        start(need)
        asked.append((node, need))
    node_rows(0, data_ref.at[0])

    col_index = lax.broadcasted_iota(jnp.int32, (TILE, positions), 0)
    even_index = lax.broadcasted_iota(jnp.int32, (pairs, positions), 0) * 2

    def weights(j, i):
        cells = data_ref[j, pl.ds(i, 1), :].astype(jnp.int32)
        east_frac = data_ref[j, pl.ds(per_band + i, 1), :]
        upper = data_ref[j, pl.ds(2 * per_band + i, 1), :]
        lower = data_ref[j, pl.ds(3 * per_band + i, 1), :]
        col_first = cells % TILE
        row_first = cells // TILE
        colw_ref[j * per_band + i] = jnp.where(
            col_index == col_first, 1.0 - east_frac,
            jnp.where(col_index == col_first + 1, east_frac, 0.0),
        ).astype(jnp.bfloat16)
        for h in range(2):
            row = even_index + h
            roww_ref[j * per_band + i, h] = jnp.where(
                row == row_first, upper, jnp.where(row == row_first + 1, lower, 0.0)
            )

    def await_asked(j):
        node, need = asked[j - 1]
        need.wait_recv()
        local = pltpu.make_async_copy(
            need_in_ref.at[j - 1], need_smem.at[j - 1], need_local.at[j]
        )
        local.start()
        node.wait_recv()
        local.wait()

    def sweep():
        surf_ref[pl.ds(HALO, length), :] = elev_ref[...]
        ground_ref[pl.ds(HALO, length), :] = bed_ref[...]
        for copy in halo:
            copy.wait_recv()
        surface = surf_ref[...]
        ground = ground_ref[...]
        rows = length + 2 * HALO
        row = lax.broadcasted_iota(jnp.int32, (rows, LANES), 0)
        lane = lax.broadcasted_iota(jnp.int32, (rows, LANES), 1)
        wall = ((row == HALO - 1) & (lane == LANES - 1) & (dom == 0)) | (
            (row == HALO + length - 1) & (lane == LANES - 1) & (dom == holders - 1)
        )

        def shifted(values, by):
            turned = pltpu.roll(values, by % LANES, 1)
            other = pltpu.roll(turned, by % rows, 0)
            edge = lane == (0 if by == 1 else LANES - 1)
            return jnp.where(edge, other, turned)

        for _ in range(SWEEPS):
            wet = jnp.maximum(surface - ground, 0.0)
            drop = surface - shifted(surface, -1)
            upwind = jnp.where(drop >= 0.0, wet, shifted(wet, -1))
            flux = jnp.where(wall, 0.0, KAPPA * upwind * drop)
            surface = surface - (flux - shifted(flux, 1))
        surf_ref[...] = surface

    own_work = [functools.partial(weights, 0, i) for i in range(per_band)]
    work = [sweep]
    for j in range(1, groups):
        work.append(functools.partial(await_asked, j))
        work += [functools.partial(weights, j, i) for i in range(per_band)]
    for item in own_work:
        item()

    events = [
        [(way, far, t) for way, t in first if far <= reach(way, t)]
        for far in range(1, half + 1)
    ]
    done = 0
    for n, batch in enumerate(events):
        for way, far, t in batch:
            ring_arrival(way, far, t).wait_recv()
            if far < reach(way, t):
                start(ring_copy(way, far + 1, t))
            start(sibling_copy(way, far, t, core))
        until = len(work) if n == half - 1 else (n + 1) * len(work) // max(half - 1, 1)
        for item in work[done:until]:
            item()
        done = max(done, until)
    for t in range(tiles_dev):
        sibling_copy(0, 0, t, 1 - core).wait_recv()
    for way, far, t in sum(events, []):
        sibling_copy(way, far, t, 1 - core).wait_recv()

    chunk = 256

    def node_values(j, i, tile):
        cells = grid_ref[lax.rem(tile, band)]
        slot = j * per_band + i
        parts = []
        for n in range(positions // chunk):
            cut = pl.ds(n * chunk, chunk)
            total = None
            for h in range(2):
                spread = jnp.dot(
                    cells[:, h * TILE : (h + 1) * TILE], colw_ref[slot, :, cut],
                    preferred_element_type=jnp.float32,
                )
                part = spread.reshape(fields, pairs, chunk) * roww_ref[slot, h, :, cut][None]
                total = part if total is None else total + part
            parts.append(jnp.sum(total, axis=1))
        return jnp.concatenate(parts, axis=1)

    def keep_forcing(slot, value):
        for f in range(fields):
            value_ref[f, pl.ds(slot, 1), :] = value[f : f + 1]

    def keep_pressure(slot, pressure):
        for m in range(positions // LANES):
            press_ref[pl.ds(slot * (positions // LANES) + m, 1), :] = pressure[
                :, m * LANES : (m + 1) * LANES
            ]

    answers = []
    for j in range(1, groups):
        for m in range(per_band // 2):
            rows = []
            for i in (2 * m, 2 * m + 1):
                value = node_values(j, i, need_smem[j - 1, i, 0])
                pressure = value[fields - 1 : fields]
                rest = pressure - pressure.astype(jnp.bfloat16).astype(jnp.float32)
                rows += [value, rest, jnp.zeros((8 - fields - 1, positions), jnp.float32)]
            res_out_ref[j - 1, m] = jnp.concatenate(rows, axis=0).astype(jnp.bfloat16)
            copy = pltpu.make_async_remote_copy(
                src_ref=res_out_ref.at[j - 1, m], dst_ref=res_in_ref.at[j - 1, m],
                send_sem=res_send.at[j - 1, m], recv_sem=res_recv.at[j - 1, m],
                device_id={"own": (own + groups - j) % groups},
            )
            start(copy)
            answers.append((j, m, copy))
    for i in range(per_band):
        slot = own * per_band + i
        value = node_values(0, i, need_ref[0, slot])
        keep_forcing(slot, value)
        keep_pressure(slot, value[fields - 1 : fields])
    for j, m, copy in answers:
        copy.wait_recv()
        got = res_in_ref[j - 1, m].astype(jnp.float32)
        for i in range(2):
            slot = (own + j) % groups * per_band + 2 * m + i
            keep_forcing(slot, got[8 * i : 8 * i + fields])
            keep_pressure(
                slot, got[8 * i + fields - 1 : 8 * i + fields] + got[8 * i + fields : 8 * i + fields + 1]
            )
    forcing_ref[...] = value_ref[...].astype(jnp.bfloat16)
    surface = surf_ref[pl.ds(HALO, length), :]
    surge_ref[...] = surface - 0.5 * press_ref[...] * jnp.clip(surface - bed_ref[...], 0.0, 1.0)
    for copy in sent:
        copy.wait_send()


def shards(
    background, storm_track, need_tiles, node_cells, node_fracs, slot_count, elevation, bed_level
):
    groups = lax.axis_size("own")
    holders = lax.axis_size("dom")
    tiles_dev, fields, cell_count = background.shape
    slots, positions = node_cells.shape
    per_band = slots // groups
    chips = holders // 2
    half = chips // 2
    pairs = cell_count // LANES
    length = elevation.shape[1] // LANES
    others = max(groups - 1, 1)
    vmem = pl.BlockSpec(memory_space=pltpu.VMEM)
    smem = pl.BlockSpec(memory_space=pltpu.SMEM)
    dma = pltpu.SemaphoreType.DMA
    forcing, surge = pl.pallas_call(
        functools.partial(kernel, groups, holders),
        out_shape=(
            jax.ShapeDtypeStruct((fields, slots, positions), jnp.bfloat16),
            jax.ShapeDtypeStruct((length, LANES), jnp.float32),
        ),
        in_specs=[smem] * 3 + [vmem] * 5,
        out_specs=(vmem, vmem),
        scratch_shapes=[
            pltpu.VMEM((tiles_dev * holders, fields * pairs, LANES), jnp.bfloat16),
            pltpu.VMEM((fields * pairs * tiles_dev, LANES), jnp.float32),
            pltpu.VMEM((groups, 4 * per_band, positions), jnp.float32),
            pltpu.VMEM((others, 4 * per_band, positions), jnp.float32),
            pltpu.VMEM((others, 8, LANES), jnp.int32),
            pltpu.VMEM((others, 8, LANES), jnp.int32),
            pltpu.SMEM((others, 8, LANES), jnp.int32),
            pltpu.VMEM((slots, TILE, positions), jnp.bfloat16),
            pltpu.VMEM((slots, 2, pairs, positions), jnp.float32),
            pltpu.VMEM((length + 2 * HALO, LANES), jnp.float32),
            pltpu.VMEM((length + 2 * HALO, LANES), jnp.float32),
            pltpu.VMEM((length, LANES), jnp.float32),
            pltpu.VMEM((fields, slots, positions), jnp.float32),
            pltpu.VMEM((others, per_band // 2, 16, positions), jnp.bfloat16),
            pltpu.VMEM((others, per_band // 2, 16, positions), jnp.bfloat16),
            dma((2, half, tiles_dev)), dma((2, half, tiles_dev)),
            dma((2, half + 1, tiles_dev)), dma((2, half + 1, tiles_dev)),
            dma((2, 2)), dma((2, 2)),
            dma((groups,)), dma((groups,)),
            dma((groups,)), dma((groups,)), dma((groups,)),
            dma((others, per_band // 2)), dma((others, per_band // 2)),
        ],
        compiler_params=pltpu.CompilerParams(
            collective_id=0, has_side_effects=True, vmem_limit_bytes=48 * 1024 * 1024
        ),
    )(
        storm_track, need_tiles, slot_count,
        background.reshape(tiles_dev, fields, pairs, LANES)
        .transpose(1, 2, 0, 3)
        .reshape(fields * pairs * tiles_dev, LANES),
        node_cells, node_fracs,
        elevation.reshape(length, LANES), bed_level.reshape(length, LANES),
    )
    return forcing.transpose(1, 0, 2), surge.reshape(1, -1)


def solution(mesh):
    placed = (
        P(("own", "dom"), None, None),
        P(),
        P(("own", "dom"), None),
        P(("own", "dom"), None),
        P(None, ("own", "dom"), None),
        P(("own", "dom")),
        P("own", "dom"),
        P("own", "dom"),
    )
    return jax.shard_map(
        shards,
        mesh=mesh,
        in_specs=placed,
        out_specs=(P(("own", "dom"), None, None), P("own", "dom")),
        check_vma=False,
    )
```

```python
import functools

import jax
import jax.numpy as jnp
from jax import lax
from jax.experimental import pallas as pl
from jax.experimental.pallas import tpu as pltpu
from jax.sharding import PartitionSpec as P

TILE = 64
TCOLS = 32
SWEEPS = 4
KAPPA = 0.08
LANES = 128
HALO = 8


def kernel(
    groups, holders,
    storm_hbm, need_hbm, count_hbm, back_hbm, cells_hbm, fracs_hbm, elev_ref, bed_ref,
    forcing_ref, surge_ref,
    storm_ref, need_ref, count_ref, back_ref, cells_ref, fracs_ref, fetch_sem,
    grid_ref, field_ref, data_ref, node_out_ref, need_out_ref, need_in_ref, need_smem,
    colw_ref, roww_ref, surf_ref, ground_ref, press_ref, value_ref, res_out_ref, res_in_ref,
    ring_send, ring_recv, sib_send, sib_recv, halo_send, halo_recv,
    node_send, node_recv, need_send, need_recv, need_local, res_send, res_recv,
):
    own = lax.axis_index("own")
    dom = lax.axis_index("dom")
    tiles_dev = grid_ref.shape[0] // holders
    fields, slots, positions = forcing_ref.shape
    pairs = grid_ref.shape[1] // fields
    per_band = slots // groups
    chips = holders // 2
    half = chips // 2
    band = tiles_dev * holders

    core = dom % 2
    chip = dom // 2
    odd = chip % 2
    place = (chip // 2) * (1 - odd) + (chips - 1 - chip // 2) * odd

    def device_at(where, which_core):
        where = (where + chips) % chips
        back = where // half
        at_chip = (2 * where) * (1 - back) + (2 * (chips - 1 - where) + 1) * back
        return at_chip * 2 + which_core

    right = device_at(place + 1, core)
    left = device_at(place - 1, core)
    sibling = chip * 2 + 1 - core
    after = (dom + 1) % holders
    before = (dom + holders - 1) % holders

    length = elev_ref.shape[0]
    inner = pl.ds(HALO, length)
    fetched = [
        pltpu.make_async_copy(source, target, fetch_sem.at[n])
        for n, (source, target) in enumerate((
            (back_hbm, back_ref), (storm_hbm, storm_ref), (need_hbm, need_ref),
            (count_hbm, count_ref), (cells_hbm, cells_ref), (fracs_hbm, fracs_ref),
            (elev_ref, surf_ref.at[inner]), (bed_ref, ground_ref.at[inner]),
        ))
    ]
    for copy in fetched:
        copy.start()

    barrier = pltpu.get_barrier_semaphore()
    for neighbour in (right, left, sibling, after, before):
        pl.semaphore_signal(barrier, inc=1, device_id={"dom": neighbour})
    for j in range(1, groups):
        pl.semaphore_signal(barrier, inc=1, device_id={"own": (own + j) % groups})

    deep = pairs * tiles_dev
    deep_index = lax.broadcasted_iota(jnp.int32, (deep, LANES), 0)
    lane_index = lax.broadcasted_iota(jnp.int32, (deep, LANES), 1)
    tile = own * band + dom * tiles_dev + deep_index % tiles_dev
    cell_row = deep_index // tiles_dev * (LANES // TILE) + lane_index // TILE
    north = (tile // TCOLS * TILE + cell_row).astype(jnp.float32)
    east = (tile % TCOLS * TILE + lane_index % TILE).astype(jnp.float32)
    for copy in fetched[:2]:
        copy.wait()
    for k in range(2):
        offset_x = east - storm_ref[k, 0]
        offset_y = north - storm_ref[k, 1]
        deficit = storm_ref[k, 2]
        shape = storm_ref[k, 4]
        radius = jnp.sqrt(offset_x * offset_x + offset_y * offset_y + 1.0)
        ratio = jnp.exp(shape * jnp.log(storm_ref[k, 3] / radius))
        decay = jnp.exp(-ratio)
        speed = jnp.sqrt(shape * deficit * ratio * decay) / radius
        added = (-speed * offset_y, speed * offset_x, -deficit * (1.0 - decay))
        for m, term in enumerate(added):
            rows = pl.ds((3 * k + m) * deep, deep)
            field_ref[rows, :] = back_ref[rows, :].astype(jnp.float32) + term
    for t in range(tiles_dev):
        grid_ref[dom * tiles_dev + t] = field_ref[
            pl.ds(t, fields * pairs, stride=tiles_dev), :
        ].astype(jnp.bfloat16)

    pl.semaphore_wait(barrier, 5 + groups - 1)

    def tile_of(where, which_core, t):
        return grid_ref.at[device_at(where, which_core) * tiles_dev + t]

    def ring_copy(way, far, t):
        where = place - far + 1 if way == 0 else place + far - 1
        ref = tile_of(where, core, t)
        return pltpu.make_async_remote_copy(
            src_ref=ref, dst_ref=ref,
            send_sem=ring_send.at[way, far - 1, t], recv_sem=ring_recv.at[way, far - 1, t],
            device_id={"dom": right if way == 0 else left},
        )

    def ring_arrival(way, far, t):
        where = place - far if way == 0 else place + far
        ref = tile_of(where, core, t)
        return pltpu.make_async_remote_copy(
            src_ref=ref, dst_ref=ref,
            send_sem=ring_send.at[way, far - 1, t], recv_sem=ring_recv.at[way, far - 1, t],
            device_id={"dom": right if way == 0 else left},
        )

    def sibling_copy(way, far, t, which_core):
        where = place - far if way == 0 else place + far
        ref = tile_of(where, which_core, t)
        return pltpu.make_async_remote_copy(
            src_ref=ref, dst_ref=ref,
            send_sem=sib_send.at[way, far, t], recv_sem=sib_recv.at[way, far, t],
            device_id={"dom": sibling},
        )

    def reach(way, t):
        return half if t % 2 == way else half - 1

    sent = []

    def start(copy):
        copy.start()
        sent.append(copy)

    first = [(way, (way + s) % tiles_dev) for s in range(tiles_dev) for way in range(2)]
    for way, t in first:
        if reach(way, t) >= 1:
            start(ring_copy(way, 1, t))
    for t in range(tiles_dev):
        start(sibling_copy(0, 0, t, core))

    ends = ((after, length - HALO, 0, 0), (before, 0, HALO + length, 1))
    halo = []
    for target, source_row, target_row, side in ends:
        for m, (source, target_ref) in enumerate(((elev_ref, surf_ref), (bed_ref, ground_ref))):
            copy = pltpu.make_async_remote_copy(
                src_ref=source.at[pl.ds(source_row, HALO)],
                dst_ref=target_ref.at[pl.ds(target_row, HALO)],
                send_sem=halo_send.at[side, m], recv_sem=halo_recv.at[side, m],
                device_id={"dom": target},
            )
            start(copy)
            halo.append(copy)

    live_index = lax.broadcasted_iota(jnp.int32, (1, positions), 1)
    row_index = lax.broadcasted_iota(jnp.int32, (8, LANES), 0)

    def node_rows(j, target):
        group = (own + j) % groups
        for i in range(per_band):
            slot = group * per_band + i
            live = live_index < count_ref[0, slot]
            north_frac = fracs_ref[1, pl.ds(slot, 1), :]
            target[pl.ds(i, 1), :] = cells_ref[pl.ds(slot, 1), :].astype(jnp.float32)
            target[pl.ds(per_band + i, 1), :] = fracs_ref[0, pl.ds(slot, 1), :]
            target[pl.ds(2 * per_band + i, 1), :] = jnp.where(live, 1.0 - north_frac, 0.0)
            target[pl.ds(3 * per_band + i, 1), :] = jnp.where(live, north_frac, 0.0)

    for copy in fetched[2:6]:
        copy.wait()
    asked = []
    for j in range(1, groups):
        group = (own + j) % groups
        node_rows(j, node_out_ref.at[j - 1])
        wanted = jnp.zeros((8, LANES), jnp.int32)
        for i in range(per_band):
            wanted = jnp.where(row_index == i, need_ref[0, group * per_band + i], wanted)
        need_out_ref[j - 1] = wanted
        node = pltpu.make_async_remote_copy(
            src_ref=node_out_ref.at[j - 1], dst_ref=data_ref.at[j],
            send_sem=node_send.at[j], recv_sem=node_recv.at[j],
            device_id={"own": group},
        )
        start(node)
        need = pltpu.make_async_remote_copy(
            src_ref=need_out_ref.at[j - 1], dst_ref=need_in_ref.at[j - 1],
            send_sem=need_send.at[j], recv_sem=need_recv.at[j],
            device_id={"own": group},
        )
        start(need)
        asked.append((node, need))
    node_rows(0, data_ref.at[0])

    col_index = lax.broadcasted_iota(jnp.int32, (TILE, positions), 0)
    even_index = lax.broadcasted_iota(jnp.int32, (pairs, positions), 0) * 2

    def weights(j, i):
        cells = data_ref[j, pl.ds(i, 1), :].astype(jnp.int32)
        east_frac = data_ref[j, pl.ds(per_band + i, 1), :]
        upper = data_ref[j, pl.ds(2 * per_band + i, 1), :]
        lower = data_ref[j, pl.ds(3 * per_band + i, 1), :]
        col_first = cells % TILE
        row_first = cells // TILE
        colw_ref[j * per_band + i] = jnp.where(
            col_index == col_first, 1.0 - east_frac,
            jnp.where(col_index == col_first + 1, east_frac, 0.0),
        ).astype(jnp.bfloat16)
        for h in range(2):
            row = even_index + h
            roww_ref[j * per_band + i, h] = jnp.where(
                row == row_first, upper, jnp.where(row == row_first + 1, lower, 0.0)
            )

    def await_asked(j):
        node, need = asked[j - 1]
        need.wait_recv()
        local = pltpu.make_async_copy(
            need_in_ref.at[j - 1], need_smem.at[j - 1], need_local.at[j]
        )
        local.start()
        node.wait_recv()
        local.wait()

    def sweep():
        for copy in fetched[6:]:
            copy.wait()
        for copy in halo:
            copy.wait_recv()
        surface = surf_ref[...]
        ground = ground_ref[...]
        rows = length + 2 * HALO
        row = lax.broadcasted_iota(jnp.int32, (rows, LANES), 0)
        lane = lax.broadcasted_iota(jnp.int32, (rows, LANES), 1)
        wall = ((row == HALO - 1) & (lane == LANES - 1) & (dom == 0)) | (
            (row == HALO + length - 1) & (lane == LANES - 1) & (dom == holders - 1)
        )

        def shifted(values, by):
            turned = pltpu.roll(values, by % LANES, 1)
            other = pltpu.roll(turned, by % rows, 0)
            edge = lane == (0 if by == 1 else LANES - 1)
            return jnp.where(edge, other, turned)

        for _ in range(SWEEPS):
            wet = jnp.maximum(surface - ground, 0.0)
            drop = surface - shifted(surface, -1)
            upwind = jnp.where(drop >= 0.0, wet, shifted(wet, -1))
            flux = jnp.where(wall, 0.0, KAPPA * upwind * drop)
            surface = surface - (flux - shifted(flux, 1))
        surf_ref[...] = surface

    own_work = [functools.partial(weights, 0, i) for i in range(per_band)]
    work = [sweep]
    for j in range(1, groups):
        work.append(functools.partial(await_asked, j))
        work += [functools.partial(weights, j, i) for i in range(per_band)]
    for item in own_work:
        item()

    events = [
        [(way, far, t) for way, t in first if far <= reach(way, t)]
        for far in range(1, half + 1)
    ]
    done = 0
    for n, batch in enumerate(events):
        for way, far, t in batch:
            ring_arrival(way, far, t).wait_recv()
            if far < reach(way, t):
                start(ring_copy(way, far + 1, t))
            start(sibling_copy(way, far, t, core))
        until = len(work) if n == half - 1 else (n + 1) * len(work) // max(half - 1, 1)
        for item in work[done:until]:
            item()
        done = max(done, until)
    for t in range(tiles_dev):
        sibling_copy(0, 0, t, 1 - core).wait_recv()
    for way, far, t in sum(events, []):
        sibling_copy(way, far, t, 1 - core).wait_recv()

    chunk = 256

    def node_values(j, i, tile):
        cells = grid_ref[lax.rem(tile, band)]
        slot = j * per_band + i
        parts = []
        for n in range(positions // chunk):
            cut = pl.ds(n * chunk, chunk)
            total = None
            for h in range(2):
                spread = jnp.dot(
                    cells[:, h * TILE : (h + 1) * TILE], colw_ref[slot, :, cut],
                    preferred_element_type=jnp.float32,
                )
                part = spread.reshape(fields, pairs, chunk) * roww_ref[slot, h, :, cut][None]
                total = part if total is None else total + part
            parts.append(jnp.sum(total, axis=1))
        return jnp.concatenate(parts, axis=1)

    def keep_forcing(slot, value):
        for f in range(fields):
            value_ref[f, pl.ds(slot, 1), :] = value[f : f + 1]

    def keep_pressure(slot, pressure):
        for m in range(positions // LANES):
            press_ref[pl.ds(slot * (positions // LANES) + m, 1), :] = pressure[
                :, m * LANES : (m + 1) * LANES
            ]

    answers = []
    for j in range(1, groups):
        for m in range(per_band // 2):
            rows = []
            for i in (2 * m, 2 * m + 1):
                value = node_values(j, i, need_smem[j - 1, i, 0])
                pressure = value[fields - 1 : fields]
                rest = pressure - pressure.astype(jnp.bfloat16).astype(jnp.float32)
                rows += [value, rest, jnp.zeros((8 - fields - 1, positions), jnp.float32)]
            res_out_ref[j - 1, m] = jnp.concatenate(rows, axis=0).astype(jnp.bfloat16)
            copy = pltpu.make_async_remote_copy(
                src_ref=res_out_ref.at[j - 1, m], dst_ref=res_in_ref.at[j - 1, m],
                send_sem=res_send.at[j - 1, m], recv_sem=res_recv.at[j - 1, m],
                device_id={"own": (own + groups - j) % groups},
            )
            start(copy)
            answers.append((j, m, copy))
    for i in range(per_band):
        slot = own * per_band + i
        value = node_values(0, i, need_ref[0, slot])
        keep_forcing(slot, value)
        keep_pressure(slot, value[fields - 1 : fields])
    for j, m, copy in answers:
        copy.wait_recv()
        got = res_in_ref[j - 1, m].astype(jnp.float32)
        for i in range(2):
            slot = (own + j) % groups * per_band + 2 * m + i
            keep_forcing(slot, got[8 * i : 8 * i + fields])
            keep_pressure(
                slot, got[8 * i + fields - 1 : 8 * i + fields] + got[8 * i + fields : 8 * i + fields + 1]
            )
    forcing_ref[...] = value_ref[...].astype(jnp.bfloat16)
    surface = surf_ref[inner, :]
    surge_ref[...] = surface - 0.5 * press_ref[...] * jnp.clip(
        surface - ground_ref[inner, :], 0.0, 1.0
    )
    for copy in sent:
        copy.wait_send()


def shards(
    background, storm_track, need_tiles, node_cells, node_fracs, slot_count, elevation, bed_level
):
    groups = lax.axis_size("own")
    holders = lax.axis_size("dom")
    tiles_dev, fields, cell_count = background.shape
    slots, positions = node_cells.shape
    per_band = slots // groups
    chips = holders // 2
    half = chips // 2
    pairs = cell_count // LANES
    length = elevation.shape[1] // LANES
    others = max(groups - 1, 1)
    vmem = pl.BlockSpec(memory_space=pltpu.VMEM)
    hbm = pl.BlockSpec(memory_space=pltpu.HBM)
    dma = pltpu.SemaphoreType.DMA
    forcing, surge = pl.pallas_call(
        functools.partial(kernel, groups, holders),
        out_shape=(
            jax.ShapeDtypeStruct((fields, slots, positions), jnp.bfloat16),
            jax.ShapeDtypeStruct((length, LANES), jnp.float32),
        ),
        in_specs=[hbm] * 8,
        out_specs=(vmem, vmem),
        scratch_shapes=[
            pltpu.SMEM(storm_track.shape, jnp.float32),
            pltpu.SMEM((1, slots), jnp.int32),
            pltpu.SMEM((1, slots), jnp.int32),
            pltpu.VMEM((fields * pairs * tiles_dev, LANES), jnp.bfloat16),
            pltpu.VMEM((slots, positions), jnp.int32),
            pltpu.VMEM((2, slots, positions), jnp.float32),
            dma((8,)),
            pltpu.VMEM((tiles_dev * holders, fields * pairs, LANES), jnp.bfloat16),
            pltpu.VMEM((fields * pairs * tiles_dev, LANES), jnp.float32),
            pltpu.VMEM((groups, 4 * per_band, positions), jnp.float32),
            pltpu.VMEM((others, 4 * per_band, positions), jnp.float32),
            pltpu.VMEM((others, 8, LANES), jnp.int32),
            pltpu.VMEM((others, 8, LANES), jnp.int32),
            pltpu.SMEM((others, 8, LANES), jnp.int32),
            pltpu.VMEM((slots, TILE, positions), jnp.bfloat16),
            pltpu.VMEM((slots, 2, pairs, positions), jnp.float32),
            pltpu.VMEM((length + 2 * HALO, LANES), jnp.float32),
            pltpu.VMEM((length + 2 * HALO, LANES), jnp.float32),
            pltpu.VMEM((length, LANES), jnp.float32),
            pltpu.VMEM((fields, slots, positions), jnp.float32),
            pltpu.VMEM((others, per_band // 2, 16, positions), jnp.bfloat16),
            pltpu.VMEM((others, per_band // 2, 16, positions), jnp.bfloat16),
            dma((2, half, tiles_dev)), dma((2, half, tiles_dev)),
            dma((2, half + 1, tiles_dev)), dma((2, half + 1, tiles_dev)),
            dma((2, 2)), dma((2, 2)),
            dma((groups,)), dma((groups,)),
            dma((groups,)), dma((groups,)), dma((groups,)),
            dma((others, per_band // 2)), dma((others, per_band // 2)),
        ],
        compiler_params=pltpu.CompilerParams(
            collective_id=0, has_side_effects=True, vmem_limit_bytes=60 * 1024 * 1024
        ),
    )(
        storm_track, need_tiles, slot_count.reshape(1, slots),
        background.reshape(tiles_dev, fields, pairs, LANES)
        .transpose(1, 2, 0, 3)
        .reshape(fields * pairs * tiles_dev, LANES),
        node_cells, node_fracs,
        elevation.reshape(length, LANES), bed_level.reshape(length, LANES),
    )
    return forcing.transpose(1, 0, 2), surge.reshape(1, -1)


def solution(mesh):
    placed = (
        P(("own", "dom"), None, None),
        P(),
        P(("own", "dom"), None),
        P(("own", "dom"), None),
        P(None, ("own", "dom"), None),
        P(("own", "dom")),
        P("own", "dom"),
        P("own", "dom"),
    )
    return jax.shard_map(
        shards,
        mesh=mesh,
        in_specs=placed,
        out_specs=(P(("own", "dom"), None, None), P("own", "dom")),
        check_vma=False,
    )
```

```python
import functools

import jax
import jax.numpy as jnp
from jax import lax
from jax.experimental import pallas as pl
from jax.experimental.pallas import tpu as pltpu
from jax.sharding import PartitionSpec as P

TILE = 64
TCOLS = 32
SWEEPS = 4
KAPPA = 0.08
LANES = 128
HALO = 8


def kernel(
    groups, holders,
    storm_hbm, need_hbm, count_hbm, back_hbm, cells_hbm, fracs_hbm, elev_ref, bed_ref,
    forcing_ref, surge_ref,
    storm_ref, need_ref, count_ref, back_ref, cells_ref, fracs_ref, fetch_sem,
    grid_ref, field_ref, data_ref, node_out_ref, need_out_ref, need_in_ref, need_smem,
    colw_ref, roww_ref, surf_ref, ground_ref, press_ref, value_ref, res_out_ref, res_in_ref,
    ring_send, ring_recv, sib_send, sib_recv, halo_send, halo_recv,
    node_send, node_recv, need_send, need_recv, need_local, res_send, res_recv,
):
    own = lax.axis_index("own")
    dom = lax.axis_index("dom")
    tiles_dev = grid_ref.shape[0] // holders
    fields, slots, positions = forcing_ref.shape
    pairs = grid_ref.shape[1] // fields
    per_band = slots // groups
    chips = holders // 2
    half = chips // 2
    band = tiles_dev * holders

    core = dom % 2
    chip = dom // 2
    odd = chip % 2
    place = (chip // 2) * (1 - odd) + (chips - 1 - chip // 2) * odd

    def device_at(where, which_core):
        where = (where + chips) % chips
        back = where // half
        at_chip = (2 * where) * (1 - back) + (2 * (chips - 1 - where) + 1) * back
        return at_chip * 2 + which_core

    right = device_at(place + 1, core)
    left = device_at(place - 1, core)
    sibling = chip * 2 + 1 - core
    after = (dom + 1) % holders
    before = (dom + holders - 1) % holders

    length = elev_ref.shape[0]
    inner = pl.ds(HALO, length)
    fetched = [
        pltpu.make_async_copy(source, target, fetch_sem.at[n])
        for n, (source, target) in enumerate((
            (back_hbm, back_ref), (storm_hbm, storm_ref), (need_hbm, need_ref),
            (count_hbm, count_ref), (cells_hbm, cells_ref), (fracs_hbm, fracs_ref),
            (elev_ref, surf_ref.at[inner]), (bed_ref, ground_ref.at[inner]),
        ))
    ]
    for copy in fetched:
        copy.start()

    barrier = pltpu.get_barrier_semaphore()
    for neighbour in (right, left, sibling, after, before):
        pl.semaphore_signal(barrier, inc=1, device_id={"dom": neighbour})
    for j in range(1, groups):
        pl.semaphore_signal(barrier, inc=1, device_id={"own": (own + j) % groups})

    deep = pairs * tiles_dev
    deep_index = lax.broadcasted_iota(jnp.int32, (deep, LANES), 0)
    lane_index = lax.broadcasted_iota(jnp.int32, (deep, LANES), 1)
    tile = own * band + dom * tiles_dev + deep_index % tiles_dev
    cell_row = deep_index // tiles_dev * (LANES // TILE) + lane_index // TILE
    north = (tile // TCOLS * TILE + cell_row).astype(jnp.float32)
    east = (tile % TCOLS * TILE + lane_index % TILE).astype(jnp.float32)
    for copy in fetched[:2]:
        copy.wait()
    for k in range(2):
        offset_x = east - storm_ref[k, 0]
        offset_y = north - storm_ref[k, 1]
        deficit = storm_ref[k, 2]
        shape = storm_ref[k, 4]
        radius = jnp.sqrt(offset_x * offset_x + offset_y * offset_y + 1.0)
        ratio = jnp.exp(shape * jnp.log(storm_ref[k, 3] / radius))
        decay = jnp.exp(-ratio)
        speed = jnp.sqrt(shape * deficit * ratio * decay) / radius
        added = (-speed * offset_y, speed * offset_x, -deficit * (1.0 - decay))
        for m, term in enumerate(added):
            rows = pl.ds((3 * k + m) * deep, deep)
            field_ref[rows, :] = back_ref[rows, :].astype(jnp.float32) + term
    for t in range(tiles_dev):
        grid_ref[dom * tiles_dev + t] = field_ref[
            pl.ds(t, fields * pairs, stride=tiles_dev), :
        ].astype(jnp.bfloat16)

    pl.semaphore_wait(barrier, 5 + groups - 1)

    def tile_of(where, which_core, t):
        return grid_ref.at[device_at(where, which_core) * tiles_dev + t]

    def ring_copy(way, far, t):
        where = place - far + 1 if way == 0 else place + far - 1
        ref = tile_of(where, core, t)
        return pltpu.make_async_remote_copy(
            src_ref=ref, dst_ref=ref,
            send_sem=ring_send.at[way, far - 1, t], recv_sem=ring_recv.at[way, far - 1, t],
            device_id={"dom": right if way == 0 else left},
        )

    def ring_arrival(way, far, t):
        where = place - far if way == 0 else place + far
        ref = tile_of(where, core, t)
        return pltpu.make_async_remote_copy(
            src_ref=ref, dst_ref=ref,
            send_sem=ring_send.at[way, far - 1, t], recv_sem=ring_recv.at[way, far - 1, t],
            device_id={"dom": right if way == 0 else left},
        )

    def sibling_copy(way, far, t, which_core):
        where = place - far if way == 0 else place + far
        ref = tile_of(where, which_core, t)
        return pltpu.make_async_remote_copy(
            src_ref=ref, dst_ref=ref,
            send_sem=sib_send.at[way, far, t], recv_sem=sib_recv.at[way, far, t],
            device_id={"dom": sibling},
        )

    def reach(way, t):
        return half if t % 2 == way else half - 1

    sent = []

    def start(copy):
        copy.start()
        sent.append(copy)

    waves = [[(way, (way + s) % tiles_dev) for way in range(2)] for s in range(tiles_dev)]

    def begin(wave):
        copies = [ring_copy(way, 1, t) for way, t in wave if reach(way, t) >= 1]
        for copy in copies:
            copy.start()
        return copies

    started = begin(waves[0])

    ends = ((after, length - HALO, 0, 0), (before, 0, HALO + length, 1))
    halo = []
    for target, source_row, target_row, side in ends:
        for m, (source, target_ref) in enumerate(((elev_ref, surf_ref), (bed_ref, ground_ref))):
            copy = pltpu.make_async_remote_copy(
                src_ref=source.at[pl.ds(source_row, HALO)],
                dst_ref=target_ref.at[pl.ds(target_row, HALO)],
                send_sem=halo_send.at[side, m], recv_sem=halo_recv.at[side, m],
                device_id={"dom": target},
            )
            start(copy)
            halo.append(copy)

    live_index = lax.broadcasted_iota(jnp.int32, (1, positions), 1)
    row_index = lax.broadcasted_iota(jnp.int32, (8, LANES), 0)

    def node_rows(j, target):
        group = (own + j) % groups
        for i in range(per_band):
            slot = group * per_band + i
            live = live_index < count_ref[0, slot]
            north_frac = fracs_ref[1, pl.ds(slot, 1), :]
            target[pl.ds(i, 1), :] = cells_ref[pl.ds(slot, 1), :].astype(jnp.float32)
            target[pl.ds(per_band + i, 1), :] = fracs_ref[0, pl.ds(slot, 1), :]
            target[pl.ds(2 * per_band + i, 1), :] = jnp.where(live, 1.0 - north_frac, 0.0)
            target[pl.ds(3 * per_band + i, 1), :] = jnp.where(live, north_frac, 0.0)

    for copy in fetched[2:6]:
        copy.wait()
    asked = []
    for j in range(1, groups):
        group = (own + j) % groups
        node_rows(j, node_out_ref.at[j - 1])
        wanted = jnp.zeros((8, LANES), jnp.int32)
        for i in range(per_band):
            wanted = jnp.where(row_index == i, need_ref[0, group * per_band + i], wanted)
        need_out_ref[j - 1] = wanted
        node = pltpu.make_async_remote_copy(
            src_ref=node_out_ref.at[j - 1], dst_ref=data_ref.at[j],
            send_sem=node_send.at[j], recv_sem=node_recv.at[j],
            device_id={"own": group},
        )
        start(node)
        need = pltpu.make_async_remote_copy(
            src_ref=need_out_ref.at[j - 1], dst_ref=need_in_ref.at[j - 1],
            send_sem=need_send.at[j], recv_sem=need_recv.at[j],
            device_id={"own": group},
        )
        start(need)
        asked.append((node, need))
    col_index = lax.broadcasted_iota(jnp.int32, (TILE, positions), 0)
    even_index = lax.broadcasted_iota(jnp.int32, (pairs, positions), 0) * 2

    def weights(j, i):
        cells = data_ref[j, pl.ds(i, 1), :].astype(jnp.int32)
        east_frac = data_ref[j, pl.ds(per_band + i, 1), :]
        upper = data_ref[j, pl.ds(2 * per_band + i, 1), :]
        lower = data_ref[j, pl.ds(3 * per_band + i, 1), :]
        col_first = cells % TILE
        row_first = cells // TILE
        colw_ref[j * per_band + i] = jnp.where(
            col_index == col_first, 1.0 - east_frac,
            jnp.where(col_index == col_first + 1, east_frac, 0.0),
        ).astype(jnp.bfloat16)
        for h in range(2):
            row = even_index + h
            roww_ref[j * per_band + i, h] = jnp.where(
                row == row_first, upper, jnp.where(row == row_first + 1, lower, 0.0)
            )

    for n, wave in enumerate(waves):
        for copy in started:
            copy.wait_send()
        if n + 1 < tiles_dev:
            started = begin(waves[n + 1])
        if n == 0:
            for t in range(tiles_dev):
                start(sibling_copy(0, 0, t, core))
            node_rows(0, data_ref.at[0])
            for i in range(per_band // 2):
                weights(0, i)

    def await_asked(j):
        node, need = asked[j - 1]
        need.wait_recv()
        local = pltpu.make_async_copy(
            need_in_ref.at[j - 1], need_smem.at[j - 1], need_local.at[j]
        )
        local.start()
        node.wait_recv()
        local.wait()

    def sweep():
        for copy in fetched[6:]:
            copy.wait()
        for copy in halo:
            copy.wait_recv()
        surface = surf_ref[...]
        ground = ground_ref[...]
        rows = length + 2 * HALO
        row = lax.broadcasted_iota(jnp.int32, (rows, LANES), 0)
        lane = lax.broadcasted_iota(jnp.int32, (rows, LANES), 1)
        wall = ((row == HALO - 1) & (lane == LANES - 1) & (dom == 0)) | (
            (row == HALO + length - 1) & (lane == LANES - 1) & (dom == holders - 1)
        )

        def shifted(values, by):
            turned = pltpu.roll(values, by % LANES, 1)
            other = pltpu.roll(turned, by % rows, 0)
            edge = lane == (0 if by == 1 else LANES - 1)
            return jnp.where(edge, other, turned)

        for _ in range(SWEEPS):
            wet = jnp.maximum(surface - ground, 0.0)
            drop = surface - shifted(surface, -1)
            upwind = jnp.where(drop >= 0.0, wet, shifted(wet, -1))
            flux = jnp.where(wall, 0.0, KAPPA * upwind * drop)
            surface = surface - (flux - shifted(flux, 1))
        surf_ref[...] = surface

    work = [functools.partial(weights, 0, i) for i in range(per_band // 2, per_band)]
    work.append(sweep)
    for j in range(1, groups):
        work.append(functools.partial(await_asked, j))
        work += [functools.partial(weights, j, i) for i in range(per_band)]

    events = [
        [(way, far, t) for way, t in wave if far <= reach(way, t)]
        for far in range(1, half + 1)
        for wave in waves
    ]
    events = [batch for batch in events if batch]
    done = 0
    for n, batch in enumerate(events):
        for way, far, t in batch:
            ring_arrival(way, far, t).wait_recv()
            if far < reach(way, t):
                start(ring_copy(way, far + 1, t))
        for way, far, t in batch:
            start(sibling_copy(way, far, t, core))
        until = (n + 1) * len(work) // max(len(events) - 1, 1) if n + 1 < len(events) else len(work)
        for item in work[done:until]:
            item()
        done = until
    for t in range(tiles_dev):
        sibling_copy(0, 0, t, 1 - core).wait_recv()
    for way, far, t in sum(events, []):
        sibling_copy(way, far, t, 1 - core).wait_recv()

    chunk = 256

    def node_values(j, i, tile):
        cells = grid_ref[lax.rem(tile, band)]
        slot = j * per_band + i
        parts = []
        for n in range(positions // chunk):
            cut = pl.ds(n * chunk, chunk)
            total = None
            for h in range(2):
                spread = jnp.dot(
                    cells[:, h * TILE : (h + 1) * TILE], colw_ref[slot, :, cut],
                    preferred_element_type=jnp.float32,
                )
                part = spread.reshape(fields, pairs, chunk) * roww_ref[slot, h, :, cut][None]
                total = part if total is None else total + part
            parts.append(jnp.sum(total, axis=1))
        return jnp.concatenate(parts, axis=1)

    def keep_forcing(slot, value):
        for f in range(fields):
            value_ref[f, pl.ds(slot, 1), :] = value[f : f + 1]

    def keep_pressure(slot, pressure):
        for m in range(positions // LANES):
            press_ref[pl.ds(slot * (positions // LANES) + m, 1), :] = pressure[
                :, m * LANES : (m + 1) * LANES
            ]

    answers = []
    for j in range(1, groups):
        for m in range(per_band // 2):
            rows = []
            for i in (2 * m, 2 * m + 1):
                value = node_values(j, i, need_smem[j - 1, i, 0])
                pressure = value[fields - 1 : fields]
                rest = pressure - pressure.astype(jnp.bfloat16).astype(jnp.float32)
                rows += [value, rest, jnp.zeros((8 - fields - 1, positions), jnp.float32)]
            res_out_ref[j - 1, m] = jnp.concatenate(rows, axis=0).astype(jnp.bfloat16)
            copy = pltpu.make_async_remote_copy(
                src_ref=res_out_ref.at[j - 1, m], dst_ref=res_in_ref.at[j - 1, m],
                send_sem=res_send.at[j - 1, m], recv_sem=res_recv.at[j - 1, m],
                device_id={"own": (own + groups - j) % groups},
            )
            start(copy)
            answers.append((j, m, copy))
    for i in range(per_band):
        slot = own * per_band + i
        value = node_values(0, i, need_ref[0, slot])
        keep_forcing(slot, value)
        keep_pressure(slot, value[fields - 1 : fields])
    for j, m, copy in answers:
        copy.wait_recv()
        got = res_in_ref[j - 1, m].astype(jnp.float32)
        for i in range(2):
            slot = (own + j) % groups * per_band + 2 * m + i
            keep_forcing(slot, got[8 * i : 8 * i + fields])
            keep_pressure(
                slot, got[8 * i + fields - 1 : 8 * i + fields] + got[8 * i + fields : 8 * i + fields + 1]
            )
    forcing_ref[...] = value_ref[...].astype(jnp.bfloat16)
    surface = surf_ref[inner, :]
    surge_ref[...] = surface - 0.5 * press_ref[...] * jnp.clip(
        surface - ground_ref[inner, :], 0.0, 1.0
    )
    for copy in sent:
        copy.wait_send()


def hand_over(forcing_in, surge_in, forcing_out, surge_out, sem):
    copies = [
        pltpu.make_async_copy(forcing_in, forcing_out, sem.at[0]),
        pltpu.make_async_copy(surge_in, surge_out, sem.at[1]),
    ]
    for copy in copies:
        copy.start()
    for copy in copies:
        copy.wait()


def shards(
    background, storm_track, need_tiles, node_cells, node_fracs, slot_count, elevation, bed_level
):
    groups = lax.axis_size("own")
    holders = lax.axis_size("dom")
    tiles_dev, fields, cell_count = background.shape
    slots, positions = node_cells.shape
    per_band = slots // groups
    chips = holders // 2
    half = chips // 2
    pairs = cell_count // LANES
    length = elevation.shape[1] // LANES
    others = max(groups - 1, 1)
    vmem = pl.BlockSpec(memory_space=pltpu.VMEM)
    hbm = pl.BlockSpec(memory_space=pltpu.HBM)
    dma = pltpu.SemaphoreType.DMA
    forcing, surge = pl.pallas_call(
        functools.partial(kernel, groups, holders),
        out_shape=(
            jax.ShapeDtypeStruct((fields, slots, positions), jnp.bfloat16),
            jax.ShapeDtypeStruct((length, LANES), jnp.float32),
        ),
        in_specs=[hbm] * 8,
        out_specs=(vmem, vmem),
        scratch_shapes=[
            pltpu.SMEM(storm_track.shape, jnp.float32),
            pltpu.SMEM((1, slots), jnp.int32),
            pltpu.SMEM((1, slots), jnp.int32),
            pltpu.VMEM((fields * pairs * tiles_dev, LANES), jnp.bfloat16),
            pltpu.VMEM((slots, positions), jnp.int32),
            pltpu.VMEM((2, slots, positions), jnp.float32),
            dma((8,)),
            pltpu.VMEM((tiles_dev * holders, fields * pairs, LANES), jnp.bfloat16),
            pltpu.VMEM((fields * pairs * tiles_dev, LANES), jnp.float32),
            pltpu.VMEM((groups, 4 * per_band, positions), jnp.float32),
            pltpu.VMEM((others, 4 * per_band, positions), jnp.float32),
            pltpu.VMEM((others, 8, LANES), jnp.int32),
            pltpu.VMEM((others, 8, LANES), jnp.int32),
            pltpu.SMEM((others, 8, LANES), jnp.int32),
            pltpu.VMEM((slots, TILE, positions), jnp.bfloat16),
            pltpu.VMEM((slots, 2, pairs, positions), jnp.float32),
            pltpu.VMEM((length + 2 * HALO, LANES), jnp.float32),
            pltpu.VMEM((length + 2 * HALO, LANES), jnp.float32),
            pltpu.VMEM((length, LANES), jnp.float32),
            pltpu.VMEM((fields, slots, positions), jnp.float32),
            pltpu.VMEM((others, per_band // 2, 16, positions), jnp.bfloat16),
            pltpu.VMEM((others, per_band // 2, 16, positions), jnp.bfloat16),
            dma((2, half, tiles_dev)), dma((2, half, tiles_dev)),
            dma((2, half + 1, tiles_dev)), dma((2, half + 1, tiles_dev)),
            dma((2, 2)), dma((2, 2)),
            dma((groups,)), dma((groups,)),
            dma((groups,)), dma((groups,)), dma((groups,)),
            dma((others, per_band // 2)), dma((others, per_band // 2)),
        ],
        compiler_params=pltpu.CompilerParams(
            collective_id=0, has_side_effects=True, vmem_limit_bytes=60 * 1024 * 1024
        ),
    )(
        storm_track, need_tiles, slot_count.reshape(1, slots),
        background.reshape(tiles_dev, fields, pairs, LANES)
        .transpose(1, 2, 0, 3)
        .reshape(fields * pairs * tiles_dev, LANES),
        node_cells, node_fracs,
        elevation.reshape(length, LANES), bed_level.reshape(length, LANES),
    )
    forcing, surge = pl.pallas_call(
        hand_over,
        out_shape=(
            jax.ShapeDtypeStruct(forcing.shape, forcing.dtype),
            jax.ShapeDtypeStruct(surge.shape, surge.dtype),
        ),
        in_specs=[hbm] * 2,
        out_specs=(hbm, hbm),
        scratch_shapes=[dma((2,))],
        compiler_params=pltpu.CompilerParams(vmem_limit_bytes=60 * 1024 * 1024),
    )(forcing, surge)
    return forcing.transpose(1, 0, 2), surge.reshape(1, -1)


def solution(mesh):
    placed = (
        P(("own", "dom"), None, None),
        P(),
        P(("own", "dom"), None),
        P(("own", "dom"), None),
        P(None, ("own", "dom"), None),
        P(("own", "dom")),
        P("own", "dom"),
        P("own", "dom"),
    )
    return jax.shard_map(
        shards,
        mesh=mesh,
        in_specs=placed,
        out_specs=(P(("own", "dom"), None, None), P("own", "dom")),
        check_vma=False,
    )
```

```python
import functools

import jax
import jax.numpy as jnp
from jax import lax
from jax.experimental import pallas as pl
from jax.experimental.pallas import tpu as pltpu
from jax.sharding import PartitionSpec as P

TILE = 64
TCOLS = 32
SWEEPS = 4
KAPPA = 0.08
LANES = 128
HALO = 8


def kernel(
    groups, holders,
    storm_hbm, need_hbm, count_hbm, back_hbm, cells_hbm, fracs_hbm, elev_ref, bed_ref,
    forcing_ref, surge_ref,
    storm_ref, need_ref, count_ref, back_ref, cells_ref, fracs_ref, fetch_sem,
    grid_ref, field_ref, data_ref, node_out_ref, need_out_ref, need_in_ref, need_smem,
    colw_ref, roww_ref, surf_ref, ground_ref, press_ref, value_ref, res_out_ref, res_in_ref,
    ring_send, ring_recv, sib_send, sib_recv, halo_send, halo_recv,
    node_send, node_recv, need_send, need_recv, need_local, res_send, res_recv,
):
    own = lax.axis_index("own")
    dom = lax.axis_index("dom")
    tiles_dev = grid_ref.shape[0] // holders
    fields, slots, positions = forcing_ref.shape
    pairs = grid_ref.shape[1] // fields
    per_band = slots // groups
    chips = holders // 2
    half = chips // 2
    band = tiles_dev * holders

    core = dom % 2
    chip = dom // 2
    odd = chip % 2
    place = (chip // 2) * (1 - odd) + (chips - 1 - chip // 2) * odd

    def device_at(where, which_core):
        where = (where + chips) % chips
        back = where // half
        at_chip = (2 * where) * (1 - back) + (2 * (chips - 1 - where) + 1) * back
        return at_chip * 2 + which_core

    right = device_at(place + 1, core)
    left = device_at(place - 1, core)
    sibling = chip * 2 + 1 - core
    after = (dom + 1) % holders
    before = (dom + holders - 1) % holders

    length = elev_ref.shape[0]
    inner = pl.ds(HALO, length)
    fetched = [
        pltpu.make_async_copy(source, target, fetch_sem.at[n])
        for n, (source, target) in enumerate((
            (back_hbm, back_ref), (storm_hbm, storm_ref), (need_hbm, need_ref),
            (count_hbm, count_ref), (cells_hbm, cells_ref), (fracs_hbm, fracs_ref),
            (elev_ref, surf_ref.at[inner]), (bed_ref, ground_ref.at[inner]),
        ))
    ]
    for copy in fetched:
        copy.start()

    barrier = pltpu.get_barrier_semaphore()
    for neighbour in (right, left, sibling, after, before):
        pl.semaphore_signal(barrier, inc=1, device_id={"dom": neighbour})
    for j in range(1, groups):
        pl.semaphore_signal(barrier, inc=1, device_id={"own": (own + j) % groups})

    deep = pairs * tiles_dev
    deep_index = lax.broadcasted_iota(jnp.int32, (deep, LANES), 0)
    lane_index = lax.broadcasted_iota(jnp.int32, (deep, LANES), 1)
    tile = own * band + dom * tiles_dev + deep_index % tiles_dev
    cell_row = deep_index // tiles_dev * (LANES // TILE) + lane_index // TILE
    north = (tile // TCOLS * TILE + cell_row).astype(jnp.float32)
    east = (tile % TCOLS * TILE + lane_index % TILE).astype(jnp.float32)
    for copy in fetched[:2]:
        copy.wait()
    for k in range(2):
        offset_x = east - storm_ref[k, 0]
        offset_y = north - storm_ref[k, 1]
        deficit = storm_ref[k, 2]
        shape = storm_ref[k, 4]
        radius = jnp.sqrt(offset_x * offset_x + offset_y * offset_y + 1.0)
        ratio = jnp.exp(shape * jnp.log(storm_ref[k, 3] / radius))
        decay = jnp.exp(-ratio)
        speed = jnp.sqrt(shape * deficit * ratio * decay) / radius
        added = (-speed * offset_y, speed * offset_x, -deficit * (1.0 - decay))
        for m, term in enumerate(added):
            rows = pl.ds((3 * k + m) * deep, deep)
            field_ref[rows, :] = back_ref[rows, :].astype(jnp.float32) + term
    for t in range(tiles_dev):
        grid_ref[dom * tiles_dev + t] = field_ref[
            pl.ds(t, fields * pairs, stride=tiles_dev), :
        ].astype(jnp.bfloat16)

    pl.semaphore_wait(barrier, 5 + groups - 1)

    def tile_of(where, which_core, t):
        return grid_ref.at[device_at(where, which_core) * tiles_dev + t]

    def ring_copy(way, far, t):
        where = place - far + 1 if way == 0 else place + far - 1
        ref = tile_of(where, core, t)
        return pltpu.make_async_remote_copy(
            src_ref=ref, dst_ref=ref,
            send_sem=ring_send.at[way, far - 1, t], recv_sem=ring_recv.at[way, far - 1, t],
            device_id={"dom": right if way == 0 else left},
        )

    def ring_arrival(way, far, t):
        where = place - far if way == 0 else place + far
        ref = tile_of(where, core, t)
        return pltpu.make_async_remote_copy(
            src_ref=ref, dst_ref=ref,
            send_sem=ring_send.at[way, far - 1, t], recv_sem=ring_recv.at[way, far - 1, t],
            device_id={"dom": right if way == 0 else left},
        )

    def sibling_copy(way, far, t, which_core):
        where = place - far if way == 0 else place + far
        ref = tile_of(where, which_core, t)
        return pltpu.make_async_remote_copy(
            src_ref=ref, dst_ref=ref,
            send_sem=sib_send.at[way, far, t], recv_sem=sib_recv.at[way, far, t],
            device_id={"dom": sibling},
        )

    def reach(way, t):
        return half if t % 2 == way else half - 1

    sent = []

    def start(copy):
        copy.start()
        sent.append(copy)

    waves = [[(way, (way + s) % tiles_dev) for way in range(2)] for s in range(tiles_dev)]

    def begin(wave):
        copies = [ring_copy(way, 1, t) for way, t in wave if reach(way, t) >= 1]
        for copy in copies:
            copy.start()
        return copies

    started = begin(waves[0])

    ends = ((after, length - HALO, 0, 0), (before, 0, HALO + length, 1))
    halo = []
    for target, source_row, target_row, side in ends:
        for m, (source, target_ref) in enumerate(((elev_ref, surf_ref), (bed_ref, ground_ref))):
            copy = pltpu.make_async_remote_copy(
                src_ref=source.at[pl.ds(source_row, HALO)],
                dst_ref=target_ref.at[pl.ds(target_row, HALO)],
                send_sem=halo_send.at[side, m], recv_sem=halo_recv.at[side, m],
                device_id={"dom": target},
            )
            start(copy)
            halo.append(copy)

    live_index = lax.broadcasted_iota(jnp.int32, (1, positions), 1)
    row_index = lax.broadcasted_iota(jnp.int32, (8, LANES), 0)

    def node_rows(j, target):
        group = (own + j) % groups
        @pl.loop(0, per_band)
        def _(i):
            slot = group * per_band + i
            live = live_index < count_ref[0, slot]
            north_frac = fracs_ref[1, pl.ds(slot, 1), :]
            target[pl.ds(i, 1), :] = cells_ref[pl.ds(slot, 1), :].astype(jnp.float32)
            target[pl.ds(per_band + i, 1), :] = fracs_ref[0, pl.ds(slot, 1), :]
            target[pl.ds(2 * per_band + i, 1), :] = jnp.where(live, 1.0 - north_frac, 0.0)
            target[pl.ds(3 * per_band + i, 1), :] = jnp.where(live, north_frac, 0.0)

    for copy in fetched[2:6]:
        copy.wait()
    asked = []
    for j in range(1, groups):
        group = (own + j) % groups
        node_rows(j, node_out_ref.at[j - 1])
        wanted = jnp.zeros((8, LANES), jnp.int32)
        for i in range(per_band):
            wanted = jnp.where(row_index == i, need_ref[0, group * per_band + i], wanted)
        need_out_ref[j - 1] = wanted
        node = pltpu.make_async_remote_copy(
            src_ref=node_out_ref.at[j - 1], dst_ref=data_ref.at[j],
            send_sem=node_send.at[j], recv_sem=node_recv.at[j],
            device_id={"own": group},
        )
        start(node)
        need = pltpu.make_async_remote_copy(
            src_ref=need_out_ref.at[j - 1], dst_ref=need_in_ref.at[j - 1],
            send_sem=need_send.at[j], recv_sem=need_recv.at[j],
            device_id={"own": group},
        )
        start(need)
        asked.append((node, need))
    col_index = lax.broadcasted_iota(jnp.int32, (TILE, positions), 0)
    even_index = lax.broadcasted_iota(jnp.int32, (pairs, positions), 0) * 2

    def weights(j, i):
        cells = data_ref[j, pl.ds(i, 1), :].astype(jnp.int32)
        east_frac = data_ref[j, pl.ds(per_band + i, 1), :]
        upper = data_ref[j, pl.ds(2 * per_band + i, 1), :]
        lower = data_ref[j, pl.ds(3 * per_band + i, 1), :]
        col_first = cells % TILE
        row_first = cells // TILE
        colw_ref[j * per_band + i] = jnp.where(
            col_index == col_first, 1.0 - east_frac,
            jnp.where(col_index == col_first + 1, east_frac, 0.0),
        ).astype(jnp.bfloat16)
        for h in range(2):
            row = even_index + h
            roww_ref[j * per_band + i, h] = jnp.where(
                row == row_first, upper, jnp.where(row == row_first + 1, lower, 0.0)
            )

    def group_weights(j):
        @pl.loop(0, per_band)
        def _(i):
            weights(j, i)

    for n, wave in enumerate(waves):
        for copy in started:
            copy.wait_send()
        if n + 1 < tiles_dev:
            started = begin(waves[n + 1])
        if n == 0:
            for t in range(tiles_dev):
                start(sibling_copy(0, 0, t, core))
            node_rows(0, data_ref.at[0])
            group_weights(0)

    def await_asked(j):
        node, need = asked[j - 1]
        need.wait_recv()
        local = pltpu.make_async_copy(
            need_in_ref.at[j - 1], need_smem.at[j - 1], need_local.at[j]
        )
        local.start()
        node.wait_recv()
        local.wait()

    def sweep():
        for copy in fetched[6:]:
            copy.wait()
        for copy in halo:
            copy.wait_recv()
        surface = surf_ref[...]
        ground = ground_ref[...]
        rows = length + 2 * HALO
        row = lax.broadcasted_iota(jnp.int32, (rows, LANES), 0)
        lane = lax.broadcasted_iota(jnp.int32, (rows, LANES), 1)
        wall = ((row == HALO - 1) & (lane == LANES - 1) & (dom == 0)) | (
            (row == HALO + length - 1) & (lane == LANES - 1) & (dom == holders - 1)
        )

        def shifted(values, by):
            turned = pltpu.roll(values, by % LANES, 1)
            other = pltpu.roll(turned, by % rows, 0)
            edge = lane == (0 if by == 1 else LANES - 1)
            return jnp.where(edge, other, turned)

        for _ in range(SWEEPS):
            wet = jnp.maximum(surface - ground, 0.0)
            drop = surface - shifted(surface, -1)
            upwind = jnp.where(drop >= 0.0, wet, shifted(wet, -1))
            flux = jnp.where(wall, 0.0, KAPPA * upwind * drop)
            surface = surface - (flux - shifted(flux, 1))
        surf_ref[...] = surface

    work = [sweep]
    for j in range(1, groups):
        work.append(functools.partial(await_asked, j))
        work.append(functools.partial(group_weights, j))

    events = [
        [(way, far, t) for way, t in wave if far <= reach(way, t)]
        for far in range(1, half + 1)
        for wave in waves
    ]
    events = [batch for batch in events if batch]
    done = 0
    for n, batch in enumerate(events):
        for way, far, t in batch:
            ring_arrival(way, far, t).wait_recv()
            if far < reach(way, t):
                start(ring_copy(way, far + 1, t))
        for way, far, t in batch:
            start(sibling_copy(way, far, t, core))
        until = min(n, len(work)) if n + 1 < len(events) else len(work)
        for item in work[done:until]:
            item()
        done = until
    for t in range(tiles_dev):
        sibling_copy(0, 0, t, 1 - core).wait_recv()
    for way, far, t in sum(events, []):
        sibling_copy(way, far, t, 1 - core).wait_recv()

    chunk = 256

    def node_values(j, i, tile):
        cells = grid_ref[lax.rem(tile, band)]
        slot = j * per_band + i
        parts = []
        for n in range(positions // chunk):
            cut = pl.ds(n * chunk, chunk)
            total = None
            for h in range(2):
                spread = jnp.dot(
                    cells[:, h * TILE : (h + 1) * TILE], colw_ref[slot, :, cut],
                    preferred_element_type=jnp.float32,
                )
                part = spread.reshape(fields, pairs, chunk) * roww_ref[slot, h, :, cut][None]
                total = part if total is None else total + part
            parts.append(jnp.sum(total, axis=1))
        return jnp.concatenate(parts, axis=1)

    def keep_forcing(slot, value):
        for f in range(fields):
            value_ref[f, pl.ds(slot, 1), :] = value[f : f + 1]

    def keep_pressure(slot, pressure):
        for m in range(positions // LANES):
            press_ref[pl.ds(slot * (positions // LANES) + m, 1), :] = pressure[
                :, m * LANES : (m + 1) * LANES
            ]

    def answer(j, m):
        return pltpu.make_async_remote_copy(
            src_ref=res_out_ref.at[j - 1, m], dst_ref=res_in_ref.at[j - 1, m],
            send_sem=res_send.at[j - 1, m], recv_sem=res_recv.at[j - 1, m],
            device_id={"own": (own + groups - j) % groups},
        )

    for j in range(1, groups):

        @pl.loop(0, per_band // 2)
        def _(m):
            rows = []
            for i in range(2):
                value = node_values(j, 2 * m + i, need_smem[j - 1, 2 * m + i, 0])
                pressure = value[fields - 1 : fields]
                rest = pressure - pressure.astype(jnp.bfloat16).astype(jnp.float32)
                rows += [value, rest, jnp.zeros((8 - fields - 1, positions), jnp.float32)]
            res_out_ref[j - 1, m] = jnp.concatenate(rows, axis=0).astype(jnp.bfloat16)
            answer(j, m).start()

    @pl.loop(0, per_band)
    def _(i):
        slot = own * per_band + i
        value = node_values(0, i, need_ref[0, slot])
        keep_forcing(slot, value)
        keep_pressure(slot, value[fields - 1 : fields])

    for j in range(1, groups):

        @pl.loop(0, per_band // 2)
        def _(m):
            answer(j, m).wait_recv()
            got = res_in_ref[j - 1, m].astype(jnp.float32)
            for i in range(2):
                slot = (own + j) % groups * per_band + 2 * m + i
                value = got[8 * i : 8 * i + fields]
                keep_forcing(slot, value)
                keep_pressure(slot, value[fields - 1 :] + got[8 * i + fields : 8 * i + fields + 1])

    forcing_ref[...] = value_ref[...].astype(jnp.bfloat16)
    surface = surf_ref[inner, :]
    surge_ref[...] = surface - 0.5 * press_ref[...] * jnp.clip(
        surface - ground_ref[inner, :], 0.0, 1.0
    )
    for copy in sent:
        copy.wait_send()
    for j in range(1, groups):
        for m in range(per_band // 2):
            answer(j, m).wait_send()


def hand_over(forcing_in, surge_in, forcing_out, surge_out, sem):
    copies = [
        pltpu.make_async_copy(forcing_in, forcing_out, sem.at[0]),
        pltpu.make_async_copy(surge_in, surge_out, sem.at[1]),
    ]
    for copy in copies:
        copy.start()
    for copy in copies:
        copy.wait()


def shards(
    background, storm_track, need_tiles, node_cells, node_fracs, slot_count, elevation, bed_level
):
    groups = lax.axis_size("own")
    holders = lax.axis_size("dom")
    tiles_dev, fields, cell_count = background.shape
    slots, positions = node_cells.shape
    per_band = slots // groups
    chips = holders // 2
    half = chips // 2
    pairs = cell_count // LANES
    length = elevation.shape[1] // LANES
    others = max(groups - 1, 1)
    vmem = pl.BlockSpec(memory_space=pltpu.VMEM)
    hbm = pl.BlockSpec(memory_space=pltpu.HBM)
    dma = pltpu.SemaphoreType.DMA
    forcing, surge = pl.pallas_call(
        functools.partial(kernel, groups, holders),
        out_shape=(
            pltpu.VMEM((fields, slots, positions), jnp.bfloat16),
            pltpu.VMEM((length, LANES), jnp.float32),
        ),
        in_specs=[hbm] * 8,
        out_specs=(vmem, vmem),
        scratch_shapes=[
            pltpu.SMEM(storm_track.shape, jnp.float32),
            pltpu.SMEM((1, slots), jnp.int32),
            pltpu.SMEM((1, slots), jnp.int32),
            pltpu.VMEM((fields * pairs * tiles_dev, LANES), jnp.bfloat16),
            pltpu.VMEM((slots, positions), jnp.int32),
            pltpu.VMEM((2, slots, positions), jnp.float32),
            dma((8,)),
            pltpu.VMEM((tiles_dev * holders, fields * pairs, LANES), jnp.bfloat16),
            pltpu.VMEM((fields * pairs * tiles_dev, LANES), jnp.float32),
            pltpu.VMEM((groups, 4 * per_band, positions), jnp.float32),
            pltpu.VMEM((others, 4 * per_band, positions), jnp.float32),
            pltpu.VMEM((others, 8, LANES), jnp.int32),
            pltpu.VMEM((others, 8, LANES), jnp.int32),
            pltpu.SMEM((others, 8, LANES), jnp.int32),
            pltpu.VMEM((slots, TILE, positions), jnp.bfloat16),
            pltpu.VMEM((slots, 2, pairs, positions), jnp.float32),
            pltpu.VMEM((length + 2 * HALO, LANES), jnp.float32),
            pltpu.VMEM((length + 2 * HALO, LANES), jnp.float32),
            pltpu.VMEM((length, LANES), jnp.float32),
            pltpu.VMEM((fields, slots, positions), jnp.float32),
            pltpu.VMEM((others, per_band // 2, 16, positions), jnp.bfloat16),
            pltpu.VMEM((others, per_band // 2, 16, positions), jnp.bfloat16),
            dma((2, half, tiles_dev)), dma((2, half, tiles_dev)),
            dma((2, half + 1, tiles_dev)), dma((2, half + 1, tiles_dev)),
            dma((2, 2)), dma((2, 2)),
            dma((groups,)), dma((groups,)),
            dma((groups,)), dma((groups,)), dma((groups,)),
            dma((others, per_band // 2)), dma((others, per_band // 2)),
        ],
        compiler_params=pltpu.CompilerParams(
            collective_id=0, has_side_effects=True, vmem_limit_bytes=60 * 1024 * 1024
        ),
    )(
        storm_track, need_tiles, slot_count.reshape(1, slots),
        background.reshape(tiles_dev, fields, pairs, LANES)
        .transpose(1, 2, 0, 3)
        .reshape(fields * pairs * tiles_dev, LANES),
        node_cells, node_fracs,
        elevation.reshape(length, LANES), bed_level.reshape(length, LANES),
    )
    forcing, surge = pl.pallas_call(
        hand_over,
        out_shape=(
            jax.ShapeDtypeStruct(forcing.shape, forcing.dtype),
            jax.ShapeDtypeStruct(surge.shape, surge.dtype),
        ),
        in_specs=[vmem] * 2,
        out_specs=(hbm, hbm),
        scratch_shapes=[dma((2,))],
    )(forcing, surge)
    return forcing.transpose(1, 0, 2), surge.reshape(1, -1)


def solution(mesh):
    placed = (
        P(("own", "dom"), None, None),
        P(),
        P(("own", "dom"), None),
        P(("own", "dom"), None),
        P(None, ("own", "dom"), None),
        P(("own", "dom")),
        P("own", "dom"),
        P("own", "dom"),
    )
    return jax.shard_map(
        shards,
        mesh=mesh,
        in_specs=placed,
        out_specs=(P(("own", "dom"), None, None), P("own", "dom")),
        check_vma=False,
    )
```

```python
import functools

import jax
import jax.numpy as jnp
from jax import lax
from jax.experimental import pallas as pl
from jax.experimental.pallas import tpu as pltpu
from jax.sharding import PartitionSpec as P

TILE = 64
TCOLS = 32
SWEEPS = 4
KAPPA = 0.08
LANES = 128
HALO = 8
PARTS = 2


def kernel(
    groups, holders,
    storm_hbm, need_hbm, count_hbm, back_hbm, cells_hbm, fracs_hbm, elev_ref, bed_ref,
    forcing_ref, surge_ref,
    storm_ref, need_ref, count_ref, back_ref, cells_ref, fracs_ref, fetch_sem,
    grid_ref, field_ref, data_ref, node_out_ref, need_out_ref, need_in_ref, need_smem,
    colw_ref, roww_ref, surf_ref, ground_ref, press_ref, value_ref, res_out_ref, res_in_ref,
    ring_send, ring_recv, sib_send, sib_recv, halo_send, halo_recv,
    node_send, node_recv, need_send, need_recv, need_local, res_send, res_recv,
):
    own = lax.axis_index("own")
    dom = lax.axis_index("dom")
    tiles_dev = grid_ref.shape[0] // holders
    fields, slots, positions = forcing_ref.shape
    pairs = grid_ref.shape[1] // fields
    per_band = slots // groups
    chips = holders // 2
    half = chips // 2
    band = tiles_dev * holders

    core = dom % 2
    chip = dom // 2
    odd = chip % 2
    place = (chip // 2) * (1 - odd) + (chips - 1 - chip // 2) * odd

    def device_at(where, which_core):
        where = (where + chips) % chips
        back = where // half
        at_chip = (2 * where) * (1 - back) + (2 * (chips - 1 - where) + 1) * back
        return at_chip * 2 + which_core

    right = device_at(place + 1, core)
    left = device_at(place - 1, core)
    sibling = chip * 2 + 1 - core
    after = (dom + 1) % holders
    before = (dom + holders - 1) % holders

    length = elev_ref.shape[0]
    inner = pl.ds(HALO, length)
    fetched = [
        pltpu.make_async_copy(source, target, fetch_sem.at[n])
        for n, (source, target) in enumerate((
            (back_hbm, back_ref), (storm_hbm, storm_ref), (need_hbm, need_ref),
            (count_hbm, count_ref), (cells_hbm, cells_ref), (fracs_hbm, fracs_ref),
            (elev_ref, surf_ref.at[inner]), (bed_ref, ground_ref.at[inner]),
        ))
    ]
    for copy in fetched:
        copy.start()

    barrier = pltpu.get_barrier_semaphore()
    for neighbour in (right, left, sibling, after, before):
        pl.semaphore_signal(barrier, inc=1, device_id={"dom": neighbour})
    for j in range(1, groups):
        pl.semaphore_signal(barrier, inc=1, device_id={"own": (own + j) % groups})

    deep = pairs * tiles_dev
    deep_index = lax.broadcasted_iota(jnp.int32, (deep, LANES), 0)
    lane_index = lax.broadcasted_iota(jnp.int32, (deep, LANES), 1)
    tile = own * band + dom * tiles_dev + deep_index % tiles_dev
    cell_row = deep_index // tiles_dev * (LANES // TILE) + lane_index // TILE
    north = (tile // TCOLS * TILE + cell_row).astype(jnp.float32)
    east = (tile % TCOLS * TILE + lane_index % TILE).astype(jnp.float32)
    for copy in fetched[:2]:
        copy.wait()
    for k in range(2):
        offset_x = east - storm_ref[k, 0]
        offset_y = north - storm_ref[k, 1]
        deficit = storm_ref[k, 2]
        shape = storm_ref[k, 4]
        radius = jnp.sqrt(offset_x * offset_x + offset_y * offset_y + 1.0)
        ratio = jnp.exp(shape * jnp.log(storm_ref[k, 3] / radius))
        decay = jnp.exp(-ratio)
        speed = jnp.sqrt(shape * deficit * ratio * decay) / radius
        added = (-speed * offset_y, speed * offset_x, -deficit * (1.0 - decay))
        for m, term in enumerate(added):
            rows = pl.ds((3 * k + m) * deep, deep)
            field_ref[rows, :] = back_ref[rows, :].astype(jnp.float32) + term
    for t in range(tiles_dev):
        grid_ref[dom * tiles_dev + t] = field_ref[
            pl.ds(t, fields * pairs, stride=tiles_dev), :
        ].astype(jnp.bfloat16)

    pl.semaphore_wait(barrier, 5 + groups - 1)

    pieces = tiles_dev * PARTS
    piece_rows = grid_ref.shape[1] // PARTS

    def tile_of(where, which_core, t):
        tile = device_at(where, which_core) * tiles_dev + t // PARTS
        return grid_ref.at[tile, pl.ds(t % PARTS * piece_rows, piece_rows)]

    def ring_copy(way, far, t):
        where = place - far + 1 if way == 0 else place + far - 1
        ref = tile_of(where, core, t)
        return pltpu.make_async_remote_copy(
            src_ref=ref, dst_ref=ref,
            send_sem=ring_send.at[way, far - 1, t], recv_sem=ring_recv.at[way, far - 1, t],
            device_id={"dom": right if way == 0 else left},
        )

    def ring_arrival(way, far, t):
        where = place - far if way == 0 else place + far
        ref = tile_of(where, core, t)
        return pltpu.make_async_remote_copy(
            src_ref=ref, dst_ref=ref,
            send_sem=ring_send.at[way, far - 1, t], recv_sem=ring_recv.at[way, far - 1, t],
            device_id={"dom": right if way == 0 else left},
        )

    def sibling_copy(way, far, t, which_core):
        where = place - far if way == 0 else place + far
        ref = tile_of(where, which_core, t)
        return pltpu.make_async_remote_copy(
            src_ref=ref, dst_ref=ref,
            send_sem=sib_send.at[way, far, t], recv_sem=sib_recv.at[way, far, t],
            device_id={"dom": sibling},
        )

    def reach(way, t):
        return half if t // (pieces // 2) == way else half - 1

    sent = []

    def start(copy):
        copy.start()
        sent.append(copy)

    waves = [[(way, (way * (pieces // 2) + s) % pieces) for way in range(2)] for s in range(pieces)]
    for wave in waves:
        for way, t in wave:
            if reach(way, t) >= 1:
                start(ring_copy(way, 1, t))
    for t in range(pieces):
        start(sibling_copy(0, 0, t, core))

    ends = ((after, length - HALO, 0, 0), (before, 0, HALO + length, 1))
    halo = []
    for target, source_row, target_row, side in ends:
        for m, (source, target_ref) in enumerate(((elev_ref, surf_ref), (bed_ref, ground_ref))):
            copy = pltpu.make_async_remote_copy(
                src_ref=source.at[pl.ds(source_row, HALO)],
                dst_ref=target_ref.at[pl.ds(target_row, HALO)],
                send_sem=halo_send.at[side, m], recv_sem=halo_recv.at[side, m],
                device_id={"dom": target},
            )
            start(copy)
            halo.append(copy)

    live_index = lax.broadcasted_iota(jnp.int32, (1, positions), 1)
    row_index = lax.broadcasted_iota(jnp.int32, (8, LANES), 0)

    def node_rows(j, target):
        group = (own + j) % groups
        @pl.loop(0, per_band)
        def _(i):
            slot = group * per_band + i
            live = live_index < count_ref[0, slot]
            north_frac = fracs_ref[1, pl.ds(slot, 1), :]
            target[pl.ds(i, 1), :] = cells_ref[pl.ds(slot, 1), :].astype(jnp.float32)
            target[pl.ds(per_band + i, 1), :] = fracs_ref[0, pl.ds(slot, 1), :]
            target[pl.ds(2 * per_band + i, 1), :] = jnp.where(live, 1.0 - north_frac, 0.0)
            target[pl.ds(3 * per_band + i, 1), :] = jnp.where(live, north_frac, 0.0)

    for copy in fetched[2:6]:
        copy.wait()
    asked = []
    for j in range(1, groups):
        group = (own + j) % groups
        node_rows(j, node_out_ref.at[j - 1])
        wanted = jnp.zeros((8, LANES), jnp.int32)
        for i in range(per_band):
            wanted = jnp.where(row_index == i, need_ref[0, group * per_band + i], wanted)
        need_out_ref[j - 1] = wanted
        node = pltpu.make_async_remote_copy(
            src_ref=node_out_ref.at[j - 1], dst_ref=data_ref.at[j],
            send_sem=node_send.at[j], recv_sem=node_recv.at[j],
            device_id={"own": group},
        )
        start(node)
        need = pltpu.make_async_remote_copy(
            src_ref=need_out_ref.at[j - 1], dst_ref=need_in_ref.at[j - 1],
            send_sem=need_send.at[j], recv_sem=need_recv.at[j],
            device_id={"own": group},
        )
        start(need)
        asked.append((node, need))
    col_index = lax.broadcasted_iota(jnp.int32, (TILE, positions), 0)
    even_index = lax.broadcasted_iota(jnp.int32, (pairs, positions), 0) * 2

    def weights(j, i):
        cells = data_ref[j, pl.ds(i, 1), :].astype(jnp.int32)
        east_frac = data_ref[j, pl.ds(per_band + i, 1), :]
        upper = data_ref[j, pl.ds(2 * per_band + i, 1), :]
        lower = data_ref[j, pl.ds(3 * per_band + i, 1), :]
        col_first = cells % TILE
        row_first = cells // TILE
        colw_ref[j * per_band + i] = jnp.where(
            col_index == col_first, 1.0 - east_frac,
            jnp.where(col_index == col_first + 1, east_frac, 0.0),
        ).astype(jnp.bfloat16)
        for h in range(2):
            row = even_index + h
            roww_ref[j * per_band + i, h] = jnp.where(
                row == row_first, upper, jnp.where(row == row_first + 1, lower, 0.0)
            )

    def group_weights(j):
        @pl.loop(0, per_band)
        def _(i):
            weights(j, i)

    node_rows(0, data_ref.at[0])
    group_weights(0)

    def await_asked(j):
        node, need = asked[j - 1]
        need.wait_recv()
        local = pltpu.make_async_copy(
            need_in_ref.at[j - 1], need_smem.at[j - 1], need_local.at[j]
        )
        local.start()
        node.wait_recv()
        local.wait()

    def sweep():
        for copy in fetched[6:]:
            copy.wait()
        for copy in halo:
            copy.wait_recv()
        surface = surf_ref[...]
        ground = ground_ref[...]
        rows = length + 2 * HALO
        row = lax.broadcasted_iota(jnp.int32, (rows, LANES), 0)
        lane = lax.broadcasted_iota(jnp.int32, (rows, LANES), 1)
        wall = ((row == HALO - 1) & (lane == LANES - 1) & (dom == 0)) | (
            (row == HALO + length - 1) & (lane == LANES - 1) & (dom == holders - 1)
        )

        def shifted(values, by):
            turned = pltpu.roll(values, by % LANES, 1)
            other = pltpu.roll(turned, by % rows, 0)
            edge = lane == (0 if by == 1 else LANES - 1)
            return jnp.where(edge, other, turned)

        for _ in range(SWEEPS):
            wet = jnp.maximum(surface - ground, 0.0)
            drop = surface - shifted(surface, -1)
            upwind = jnp.where(drop >= 0.0, wet, shifted(wet, -1))
            flux = jnp.where(wall, 0.0, KAPPA * upwind * drop)
            surface = surface - (flux - shifted(flux, 1))
        surf_ref[...] = surface

    work = [sweep]
    for j in range(1, groups):
        work.append(functools.partial(await_asked, j))
        work.append(functools.partial(group_weights, j))

    events = [
        [(way, far, t) for way, t in wave if far <= reach(way, t)]
        for far in range(1, half + 1)
        for wave in waves
    ]
    events = [batch for batch in events if batch]
    done = 0
    for n, batch in enumerate(events):
        for way, far, t in batch:
            ring_arrival(way, far, t).wait_recv()
            if far < reach(way, t):
                start(ring_copy(way, far + 1, t))
        for way, far, t in batch:
            start(sibling_copy(way, far, t, core))
        until = min(n // PARTS, len(work)) if n + 1 < len(events) else len(work)
        for item in work[done:until]:
            item()
        done = until
    for t in range(pieces):
        sibling_copy(0, 0, t, 1 - core).wait_recv()
    for way, far, t in sum(events, []):
        sibling_copy(way, far, t, 1 - core).wait_recv()

    chunk = 256

    def node_values(j, i, tile):
        cells = grid_ref[lax.rem(tile, band)]
        slot = j * per_band + i
        parts = []
        for n in range(positions // chunk):
            cut = pl.ds(n * chunk, chunk)
            total = None
            for h in range(2):
                spread = jnp.dot(
                    cells[:, h * TILE : (h + 1) * TILE], colw_ref[slot, :, cut],
                    preferred_element_type=jnp.float32,
                )
                part = spread.reshape(fields, pairs, chunk) * roww_ref[slot, h, :, cut][None]
                total = part if total is None else total + part
            parts.append(jnp.sum(total, axis=1))
        return jnp.concatenate(parts, axis=1)

    def keep_forcing(slot, value):
        for f in range(fields):
            value_ref[f, pl.ds(slot, 1), :] = value[f : f + 1]

    def keep_pressure(slot, pressure):
        for m in range(positions // LANES):
            press_ref[pl.ds(slot * (positions // LANES) + m, 1), :] = pressure[
                :, m * LANES : (m + 1) * LANES
            ]

    def answer(j, m):
        return pltpu.make_async_remote_copy(
            src_ref=res_out_ref.at[j - 1, m], dst_ref=res_in_ref.at[j - 1, m],
            send_sem=res_send.at[j - 1, m], recv_sem=res_recv.at[j - 1, m],
            device_id={"own": (own + groups - j) % groups},
        )

    for j in range(1, groups):

        @pl.loop(0, per_band // 2)
        def _(m):
            rows = []
            for i in range(2):
                value = node_values(j, 2 * m + i, need_smem[j - 1, 2 * m + i, 0])
                pressure = value[fields - 1 : fields]
                rest = pressure - pressure.astype(jnp.bfloat16).astype(jnp.float32)
                rows += [value, rest, jnp.zeros((8 - fields - 1, positions), jnp.float32)]
            res_out_ref[j - 1, m] = jnp.concatenate(rows, axis=0).astype(jnp.bfloat16)
            answer(j, m).start()

    @pl.loop(0, per_band)
    def _(i):
        slot = own * per_band + i
        value = node_values(0, i, need_ref[0, slot])
        keep_forcing(slot, value)
        keep_pressure(slot, value[fields - 1 : fields])

    for j in range(1, groups):

        @pl.loop(0, per_band // 2)
        def _(m):
            answer(j, m).wait_recv()
            got = res_in_ref[j - 1, m].astype(jnp.float32)
            for i in range(2):
                slot = (own + j) % groups * per_band + 2 * m + i
                value = got[8 * i : 8 * i + fields]
                keep_forcing(slot, value)
                keep_pressure(slot, value[fields - 1 :] + got[8 * i + fields : 8 * i + fields + 1])

    forcing_ref[...] = value_ref[...].astype(jnp.bfloat16)
    surface = surf_ref[inner, :]
    surge_ref[...] = surface - 0.5 * press_ref[...] * jnp.clip(
        surface - ground_ref[inner, :], 0.0, 1.0
    )
    for copy in sent:
        copy.wait_send()
    for j in range(1, groups):
        for m in range(per_band // 2):
            answer(j, m).wait_send()


def shards(
    background, storm_track, need_tiles, node_cells, node_fracs, slot_count, elevation, bed_level
):
    groups = lax.axis_size("own")
    holders = lax.axis_size("dom")
    tiles_dev, fields, cell_count = background.shape
    slots, positions = node_cells.shape
    per_band = slots // groups
    chips = holders // 2
    half = chips // 2
    pairs = cell_count // LANES
    length = elevation.shape[1] // LANES
    others = max(groups - 1, 1)
    pieces = tiles_dev * PARTS
    vmem = pl.BlockSpec(memory_space=pltpu.VMEM)
    hbm = pl.BlockSpec(memory_space=pltpu.HBM)
    dma = pltpu.SemaphoreType.DMA
    forcing, surge = pl.pallas_call(
        functools.partial(kernel, groups, holders),
        out_shape=(
            pltpu.VMEM((fields, slots, positions), jnp.bfloat16),
            pltpu.VMEM((length, LANES), jnp.float32),
        ),
        in_specs=[hbm] * 8,
        out_specs=(vmem, vmem),
        scratch_shapes=[
            pltpu.SMEM(storm_track.shape, jnp.float32),
            pltpu.SMEM((1, slots), jnp.int32),
            pltpu.SMEM((1, slots), jnp.int32),
            pltpu.VMEM((fields * pairs * tiles_dev, LANES), jnp.bfloat16),
            pltpu.VMEM((slots, positions), jnp.int32),
            pltpu.VMEM((2, slots, positions), jnp.float32),
            dma((8,)),
            pltpu.VMEM((tiles_dev * holders, fields * pairs, LANES), jnp.bfloat16),
            pltpu.VMEM((fields * pairs * tiles_dev, LANES), jnp.float32),
            pltpu.VMEM((groups, 4 * per_band, positions), jnp.float32),
            pltpu.VMEM((others, 4 * per_band, positions), jnp.float32),
            pltpu.VMEM((others, 8, LANES), jnp.int32),
            pltpu.VMEM((others, 8, LANES), jnp.int32),
            pltpu.SMEM((others, 8, LANES), jnp.int32),
            pltpu.VMEM((slots, TILE, positions), jnp.bfloat16),
            pltpu.VMEM((slots, 2, pairs, positions), jnp.float32),
            pltpu.VMEM((length + 2 * HALO, LANES), jnp.float32),
            pltpu.VMEM((length + 2 * HALO, LANES), jnp.float32),
            pltpu.VMEM((length, LANES), jnp.float32),
            pltpu.VMEM((fields, slots, positions), jnp.float32),
            pltpu.VMEM((others, per_band // 2, 16, positions), jnp.bfloat16),
            pltpu.VMEM((others, per_band // 2, 16, positions), jnp.bfloat16),
            dma((2, half, pieces)), dma((2, half, pieces)),
            dma((2, half + 1, pieces)), dma((2, half + 1, pieces)),
            dma((2, 2)), dma((2, 2)),
            dma((groups,)), dma((groups,)),
            dma((groups,)), dma((groups,)), dma((groups,)),
            dma((others, per_band // 2)), dma((others, per_band // 2)),
        ],
        compiler_params=pltpu.CompilerParams(
            collective_id=0, has_side_effects=True, vmem_limit_bytes=60 * 1024 * 1024
        ),
    )(
        storm_track, need_tiles, slot_count.reshape(1, slots),
        background.reshape(tiles_dev, fields, pairs, LANES)
        .transpose(1, 2, 0, 3)
        .reshape(fields * pairs * tiles_dev, LANES),
        node_cells, node_fracs,
        elevation.reshape(length, LANES), bed_level.reshape(length, LANES),
    )
    return forcing.transpose(1, 0, 2), surge.reshape(1, -1)


def solution(mesh):
    placed = (
        P(("own", "dom"), None, None),
        P(),
        P(("own", "dom"), None),
        P(("own", "dom"), None),
        P(None, ("own", "dom"), None),
        P(("own", "dom")),
        P("own", "dom"),
        P("own", "dom"),
    )
    return jax.shard_map(
        shards,
        mesh=mesh,
        in_specs=placed,
        out_specs=(P(("own", "dom"), None, None), P("own", "dom")),
        check_vma=False,
    )
```

```python
import functools

import jax
import jax.numpy as jnp
from jax import lax
from jax.experimental import pallas as pl
from jax.experimental.pallas import tpu as pltpu
from jax.sharding import PartitionSpec as P

TILE = 64
TCOLS = 32
SWEEPS = 4
KAPPA = 0.08
LANES = 128
HALO = 8
PARTS = 2


def kernel(
    groups, holders,
    storm_hbm, need_hbm, count_hbm, back_hbm, cells_hbm, fracs_hbm, elev_ref, bed_ref,
    forcing_ref, surge_ref,
    storm_ref, need_ref, count_ref, back_ref, cells_ref, fracs_ref, fetch_sem,
    grid_ref, field_ref, data_ref, node_out_ref, need_out_ref, need_in_ref, need_smem,
    colw_ref, roww_ref, surf_ref, ground_ref, press_ref, value_ref, res_out_ref, res_in_ref,
    ring_send, ring_recv, sib_send, sib_recv, halo_send, halo_recv,
    node_send, node_recv, need_send, need_recv, need_local, res_send, res_recv,
):
    own = lax.axis_index("own")
    dom = lax.axis_index("dom")
    tiles_dev = grid_ref.shape[0] // holders
    fields, slots, positions = forcing_ref.shape
    pairs = grid_ref.shape[1] // fields
    per_band = slots // groups
    chips = holders // 2
    half = chips // 2
    band = tiles_dev * holders

    core = dom % 2
    chip = dom // 2
    odd = chip % 2
    place = (chip // 2) * (1 - odd) + (chips - 1 - chip // 2) * odd

    def device_at(where, which_core):
        where = (where + chips) % chips
        back = where // half
        at_chip = (2 * where) * (1 - back) + (2 * (chips - 1 - where) + 1) * back
        return at_chip * 2 + which_core

    right = device_at(place + 1, core)
    left = device_at(place - 1, core)
    sibling = chip * 2 + 1 - core
    after = (dom + 1) % holders
    before = (dom + holders - 1) % holders

    length = elev_ref.shape[0]
    inner = pl.ds(HALO, length)
    fetched = [
        pltpu.make_async_copy(source, target, fetch_sem.at[n])
        for n, (source, target) in enumerate((
            (back_hbm, back_ref), (storm_hbm, storm_ref), (need_hbm, need_ref),
            (count_hbm, count_ref), (cells_hbm, cells_ref), (fracs_hbm, fracs_ref),
            (elev_ref, surf_ref.at[inner]), (bed_ref, ground_ref.at[inner]),
        ))
    ]
    for copy in fetched:
        copy.start()

    barrier = pltpu.get_barrier_semaphore()
    for neighbour in (right, left, sibling, after, before):
        pl.semaphore_signal(barrier, inc=1, device_id={"dom": neighbour})
    for j in range(1, groups):
        pl.semaphore_signal(barrier, inc=1, device_id={"own": (own + j) % groups})

    deep = pairs * tiles_dev
    deep_index = lax.broadcasted_iota(jnp.int32, (deep, LANES), 0)
    lane_index = lax.broadcasted_iota(jnp.int32, (deep, LANES), 1)
    tile = own * band + dom * tiles_dev + deep_index % tiles_dev
    cell_row = deep_index // tiles_dev * (LANES // TILE) + lane_index // TILE
    north = (tile // TCOLS * TILE + cell_row).astype(jnp.float32)
    east = (tile % TCOLS * TILE + lane_index % TILE).astype(jnp.float32)
    for copy in fetched[:2]:
        copy.wait()
    for k in range(2):
        offset_x = east - storm_ref[k, 0]
        offset_y = north - storm_ref[k, 1]
        deficit = storm_ref[k, 2]
        shape = storm_ref[k, 4]
        radius = jnp.sqrt(offset_x * offset_x + offset_y * offset_y + 1.0)
        ratio = jnp.exp(shape * jnp.log(storm_ref[k, 3] / radius))
        decay = jnp.exp(-ratio)
        speed = jnp.sqrt(shape * deficit * ratio * decay) / radius
        added = (-speed * offset_y, speed * offset_x, -deficit * (1.0 - decay))
        for m, term in enumerate(added):
            rows = pl.ds((3 * k + m) * deep, deep)
            field_ref[rows, :] = back_ref[rows, :].astype(jnp.float32) + term
    for t in range(tiles_dev):
        grid_ref[dom * tiles_dev + t] = field_ref[
            pl.ds(t, fields * pairs, stride=tiles_dev), :
        ].astype(jnp.bfloat16)

    pl.semaphore_wait(barrier, 5 + groups - 1)

    pieces = tiles_dev * PARTS
    piece_rows = grid_ref.shape[1] // PARTS

    def tile_of(where, which_core, t):
        tile = device_at(where, which_core) * tiles_dev + t // PARTS
        return grid_ref.at[tile, pl.ds(t % PARTS * piece_rows, piece_rows)]

    def ring_copy(way, far, t):
        where = place - far + 1 if way == 0 else place + far - 1
        ref = tile_of(where, core, t)
        return pltpu.make_async_remote_copy(
            src_ref=ref, dst_ref=ref,
            send_sem=ring_send.at[way, far - 1, t], recv_sem=ring_recv.at[way, far - 1, t],
            device_id={"dom": right if way == 0 else left},
        )

    def ring_arrival(way, far, t):
        where = place - far if way == 0 else place + far
        ref = tile_of(where, core, t)
        return pltpu.make_async_remote_copy(
            src_ref=ref, dst_ref=ref,
            send_sem=ring_send.at[way, far - 1, t], recv_sem=ring_recv.at[way, far - 1, t],
            device_id={"dom": right if way == 0 else left},
        )

    def sibling_copy(way, far, t, which_core):
        where = place - far if way == 0 else place + far
        ref = tile_of(where, which_core, t)
        return pltpu.make_async_remote_copy(
            src_ref=ref, dst_ref=ref,
            send_sem=sib_send.at[way, far, t], recv_sem=sib_recv.at[way, far, t],
            device_id={"dom": sibling},
        )

    def reach(way, t):
        return half if t // (pieces // 2) == way else half - 1

    sent = []

    def start(copy):
        copy.start()
        sent.append(copy)

    waves = [[(way, (way * (pieces // 2) + s) % pieces) for way in range(2)] for s in range(pieces)]
    for wave in waves:
        for way, t in wave:
            if reach(way, t) >= 1:
                start(ring_copy(way, 1, t))
    for t in range(pieces):
        start(sibling_copy(0, 0, t, core))

    ends = ((after, length - HALO, 0, 0), (before, 0, HALO + length, 1))
    halo = []
    for target, source_row, target_row, side in ends:
        for m, (source, target_ref) in enumerate(((elev_ref, surf_ref), (bed_ref, ground_ref))):
            copy = pltpu.make_async_remote_copy(
                src_ref=source.at[pl.ds(source_row, HALO)],
                dst_ref=target_ref.at[pl.ds(target_row, HALO)],
                send_sem=halo_send.at[side, m], recv_sem=halo_recv.at[side, m],
                device_id={"dom": target},
            )
            start(copy)
            halo.append(copy)

    live_index = lax.broadcasted_iota(jnp.int32, (1, positions), 1)
    row_index = lax.broadcasted_iota(jnp.int32, (8, LANES), 0)

    def node_rows(j, target):
        group = (own + j) % groups
        @pl.loop(0, per_band)
        def _(i):
            slot = group * per_band + i
            live = live_index < count_ref[0, slot]
            north_frac = fracs_ref[1, pl.ds(slot, 1), :]
            target[pl.ds(i, 1), :] = cells_ref[pl.ds(slot, 1), :].astype(jnp.float32)
            target[pl.ds(per_band + i, 1), :] = fracs_ref[0, pl.ds(slot, 1), :]
            target[pl.ds(2 * per_band + i, 1), :] = jnp.where(live, 1.0 - north_frac, 0.0)
            target[pl.ds(3 * per_band + i, 1), :] = jnp.where(live, north_frac, 0.0)

    for copy in fetched[2:6]:
        copy.wait()
    asked = []
    for j in range(1, groups):
        group = (own + j) % groups
        node_rows(j, node_out_ref.at[j - 1])
        wanted = jnp.zeros((8, LANES), jnp.int32)
        for i in range(per_band):
            wanted = jnp.where(row_index == i, need_ref[0, group * per_band + i], wanted)
        need_out_ref[j - 1] = wanted
        node = pltpu.make_async_remote_copy(
            src_ref=node_out_ref.at[j - 1], dst_ref=data_ref.at[j],
            send_sem=node_send.at[j], recv_sem=node_recv.at[j],
            device_id={"own": group},
        )
        start(node)
        need = pltpu.make_async_remote_copy(
            src_ref=need_out_ref.at[j - 1], dst_ref=need_in_ref.at[j - 1],
            send_sem=need_send.at[j], recv_sem=need_recv.at[j],
            device_id={"own": group},
        )
        start(need)
        asked.append((node, need))
    col_index = lax.broadcasted_iota(jnp.int32, (TILE, positions), 0)
    even_index = lax.broadcasted_iota(jnp.int32, (pairs, positions), 0) * 2

    def weights(j, i):
        cells = data_ref[j, pl.ds(i, 1), :].astype(jnp.int32)
        east_frac = data_ref[j, pl.ds(per_band + i, 1), :]
        upper = data_ref[j, pl.ds(2 * per_band + i, 1), :]
        lower = data_ref[j, pl.ds(3 * per_band + i, 1), :]
        col_first = cells % TILE
        row_first = cells // TILE
        colw_ref[j * per_band + i] = jnp.where(
            col_index == col_first, 1.0 - east_frac,
            jnp.where(col_index == col_first + 1, east_frac, 0.0),
        ).astype(jnp.bfloat16)
        for h in range(2):
            row = even_index + h
            roww_ref[j * per_band + i, h] = jnp.where(
                row == row_first, upper, jnp.where(row == row_first + 1, lower, 0.0)
            )

    def some_weights(j, part):
        @pl.loop(part * (per_band // 2), (part + 1) * (per_band // 2))
        def _(i):
            weights(j, i)

    node_rows(0, data_ref.at[0])
    some_weights(0, 0)

    def await_asked(j):
        node, need = asked[j - 1]
        need.wait_recv()
        local = pltpu.make_async_copy(
            need_in_ref.at[j - 1], need_smem.at[j - 1], need_local.at[j]
        )
        local.start()
        node.wait_recv()
        local.wait()

    def sweep():
        for copy in fetched[6:]:
            copy.wait()
        for copy in halo:
            copy.wait_recv()
        surface = surf_ref[...]
        ground = ground_ref[...]
        rows = length + 2 * HALO
        row = lax.broadcasted_iota(jnp.int32, (rows, LANES), 0)
        lane = lax.broadcasted_iota(jnp.int32, (rows, LANES), 1)
        wall = ((row == HALO - 1) & (lane == LANES - 1) & (dom == 0)) | (
            (row == HALO + length - 1) & (lane == LANES - 1) & (dom == holders - 1)
        )

        def shifted(values, by):
            turned = pltpu.roll(values, by % LANES, 1)
            other = pltpu.roll(turned, by % rows, 0)
            edge = lane == (0 if by == 1 else LANES - 1)
            return jnp.where(edge, other, turned)

        for _ in range(SWEEPS):
            wet = jnp.maximum(surface - ground, 0.0)
            drop = surface - shifted(surface, -1)
            upwind = jnp.where(drop >= 0.0, wet, shifted(wet, -1))
            flux = jnp.where(wall, 0.0, KAPPA * upwind * drop)
            surface = surface - (flux - shifted(flux, 1))
        surf_ref[...] = surface

    work = [functools.partial(some_weights, 0, 1)]
    for j in range(1, groups):
        work.append(lambda j=j: (await_asked(j), some_weights(j, 0)))
        work.append(functools.partial(some_weights, j, 1))

    events = [
        [[(way, far, t) for way, t in wave if far <= reach(way, t)] for wave in waves]
        for far in range(1, half + 1)
    ]
    done = 0
    for n, hop in enumerate(events):
        for batch in hop:
            for way, far, t in batch:
                ring_arrival(way, far, t).wait_recv()
                if far < reach(way, t):
                    start(ring_copy(way, far + 1, t))
            for way, far, t in batch:
                start(sibling_copy(way, far, t, core))
        if n + 1 < half:
            until = (n + 1) * len(work) // (half - 1)
            for item in work[done:until]:
                item()
            done = until
            if n + 2 == half:
                sweep()
    if half == 1:
        for item in work + [sweep]:
            item()
    for t in range(pieces):
        sibling_copy(0, 0, t, 1 - core).wait_recv()
    for way, far, t in sum(sum(events, []), []):
        sibling_copy(way, far, t, 1 - core).wait_recv()

    chunk = 256

    def node_values(j, i, tile):
        cells = grid_ref[lax.rem(tile, band)]
        slot = j * per_band + i
        parts = []
        for n in range(positions // chunk):
            cut = pl.ds(n * chunk, chunk)
            total = None
            for h in range(2):
                spread = jnp.dot(
                    cells[:, h * TILE : (h + 1) * TILE], colw_ref[slot, :, cut],
                    preferred_element_type=jnp.float32,
                )
                part = spread.reshape(fields, pairs, chunk) * roww_ref[slot, h, :, cut][None]
                total = part if total is None else total + part
            parts.append(jnp.sum(total, axis=1))
        return jnp.concatenate(parts, axis=1)

    def keep_forcing(slot, value):
        for f in range(fields):
            value_ref[f, pl.ds(slot, 1), :] = value[f : f + 1]

    def keep_pressure(slot, pressure):
        for m in range(positions // LANES):
            press_ref[pl.ds(slot * (positions // LANES) + m, 1), :] = pressure[
                :, m * LANES : (m + 1) * LANES
            ]

    def answer(j, m):
        return pltpu.make_async_remote_copy(
            src_ref=res_out_ref.at[j - 1, m], dst_ref=res_in_ref.at[j - 1, m],
            send_sem=res_send.at[j - 1, m], recv_sem=res_recv.at[j - 1, m],
            device_id={"own": (own + groups - j) % groups},
        )

    for j in range(1, groups):

        @pl.loop(0, per_band // 2)
        def _(m):
            rows = []
            for i in range(2):
                value = node_values(j, 2 * m + i, need_smem[j - 1, 2 * m + i, 0])
                pressure = value[fields - 1 : fields]
                rest = pressure - pressure.astype(jnp.bfloat16).astype(jnp.float32)
                rows += [value, rest, jnp.zeros((8 - fields - 1, positions), jnp.float32)]
            res_out_ref[j - 1, m] = jnp.concatenate(rows, axis=0).astype(jnp.bfloat16)
            answer(j, m).start()

    @pl.loop(0, per_band)
    def _(i):
        slot = own * per_band + i
        value = node_values(0, i, need_ref[0, slot])
        keep_forcing(slot, value)
        keep_pressure(slot, value[fields - 1 : fields])

    for j in range(1, groups):

        @pl.loop(0, per_band // 2)
        def _(m):
            answer(j, m).wait_recv()
            got = res_in_ref[j - 1, m].astype(jnp.float32)
            for i in range(2):
                slot = (own + j) % groups * per_band + 2 * m + i
                value = got[8 * i : 8 * i + fields]
                keep_forcing(slot, value)
                keep_pressure(slot, value[fields - 1 :] + got[8 * i + fields : 8 * i + fields + 1])

    forcing_ref[...] = value_ref[...].astype(jnp.bfloat16)
    surface = surf_ref[inner, :]
    surge_ref[...] = surface - 0.5 * press_ref[...] * jnp.clip(
        surface - ground_ref[inner, :], 0.0, 1.0
    )
    for copy in sent:
        copy.wait_send()
    for j in range(1, groups):
        for m in range(per_band // 2):
            answer(j, m).wait_send()


def shards(
    background, storm_track, need_tiles, node_cells, node_fracs, slot_count, elevation, bed_level
):
    groups = lax.axis_size("own")
    holders = lax.axis_size("dom")
    tiles_dev, fields, cell_count = background.shape
    slots, positions = node_cells.shape
    per_band = slots // groups
    chips = holders // 2
    half = chips // 2
    pairs = cell_count // LANES
    length = elevation.shape[1] // LANES
    others = max(groups - 1, 1)
    pieces = tiles_dev * PARTS
    vmem = pl.BlockSpec(memory_space=pltpu.VMEM)
    hbm = pl.BlockSpec(memory_space=pltpu.HBM)
    dma = pltpu.SemaphoreType.DMA
    forcing, surge = pl.pallas_call(
        functools.partial(kernel, groups, holders),
        out_shape=(
            pltpu.VMEM((fields, slots, positions), jnp.bfloat16),
            pltpu.VMEM((length, LANES), jnp.float32),
        ),
        in_specs=[hbm] * 8,
        out_specs=(vmem, vmem),
        scratch_shapes=[
            pltpu.SMEM(storm_track.shape, jnp.float32),
            pltpu.SMEM((1, slots), jnp.int32),
            pltpu.SMEM((1, slots), jnp.int32),
            pltpu.VMEM((fields * pairs * tiles_dev, LANES), jnp.bfloat16),
            pltpu.VMEM((slots, positions), jnp.int32),
            pltpu.VMEM((2, slots, positions), jnp.float32),
            dma((8,)),
            pltpu.VMEM((tiles_dev * holders, fields * pairs, LANES), jnp.bfloat16),
            pltpu.VMEM((fields * pairs * tiles_dev, LANES), jnp.float32),
            pltpu.VMEM((groups, 4 * per_band, positions), jnp.float32),
            pltpu.VMEM((others, 4 * per_band, positions), jnp.float32),
            pltpu.VMEM((others, 8, LANES), jnp.int32),
            pltpu.VMEM((others, 8, LANES), jnp.int32),
            pltpu.SMEM((others, 8, LANES), jnp.int32),
            pltpu.VMEM((slots, TILE, positions), jnp.bfloat16),
            pltpu.VMEM((slots, 2, pairs, positions), jnp.float32),
            pltpu.VMEM((length + 2 * HALO, LANES), jnp.float32),
            pltpu.VMEM((length + 2 * HALO, LANES), jnp.float32),
            pltpu.VMEM((length, LANES), jnp.float32),
            pltpu.VMEM((fields, slots, positions), jnp.float32),
            pltpu.VMEM((others, per_band // 2, 16, positions), jnp.bfloat16),
            pltpu.VMEM((others, per_band // 2, 16, positions), jnp.bfloat16),
            dma((2, half, pieces)), dma((2, half, pieces)),
            dma((2, half + 1, pieces)), dma((2, half + 1, pieces)),
            dma((2, 2)), dma((2, 2)),
            dma((groups,)), dma((groups,)),
            dma((groups,)), dma((groups,)), dma((groups,)),
            dma((others, per_band // 2)), dma((others, per_band // 2)),
        ],
        compiler_params=pltpu.CompilerParams(
            collective_id=0, has_side_effects=True, vmem_limit_bytes=60 * 1024 * 1024
        ),
    )(
        storm_track, need_tiles, slot_count.reshape(1, slots),
        background.reshape(tiles_dev, fields, pairs, LANES)
        .transpose(1, 2, 0, 3)
        .reshape(fields * pairs * tiles_dev, LANES),
        node_cells, node_fracs,
        elevation.reshape(length, LANES), bed_level.reshape(length, LANES),
    )
    return forcing.transpose(1, 0, 2), surge.reshape(1, -1)


def solution(mesh):
    placed = (
        P(("own", "dom"), None, None),
        P(),
        P(("own", "dom"), None),
        P(("own", "dom"), None),
        P(None, ("own", "dom"), None),
        P(("own", "dom")),
        P("own", "dom"),
        P("own", "dom"),
    )
    return jax.shard_map(
        shards,
        mesh=mesh,
        in_specs=placed,
        out_specs=(P(("own", "dom"), None, None), P("own", "dom")),
        check_vma=False,
    )
```
